32 devices in a mesh: row: 8 (over z, x), col: 4 (over y, core).
Axes of the slice: x: 2, y: 2, z: 4, core: 2. Of those that a mesh axis runs over, the one named last changes fastest.
Arguments:
- tiles: bfloat16 [8, 4, 32, 128, 128], P('row', 'col'), may hold values from -0.375 to 0.375
- coords: int32 [8, 4, 32, 2], P('row', 'col'), may hold values from 0 to 8191, as said below
- counts: int32 [8, 4], P('row', 'col'), may hold values from 16 to 32, as said below
- rhs: float32 [2, 4194304], P(None, ('row', 'col')), may hold values from -50 to 50
Outputs:
- solution: float32 [2, 4194304], P(None, ('col', 'row'))
- phi_bar: float32 [2], replicated
The draws below stay inside these ranges and needn't reach their ends.
Inputs may be any that keep to these rules, and one draw needn't show every extreme that they name: coords[p, q, k, 0] is a local block row below 4096 and coords[p, q, k, 1] a local block column below 8192; within one tile no two slots share a block row and no two share a block column; counting all 32 slots of a tile, exactly 8 of its block rows fall in each of the 4 ranges of 1024 consecutive block rows, and exactly 4 of its block columns in each of the 8 ranges of 1024 consecutive block columns. The first counts[p, q] slots of tile (p, q) are used; some tile uses all 32.
All inputs are finite; a program needn't handle non-finite values.
Results may differ from the reference program's by a relative error of at most 0.015.
Values may be sent and summed in bfloat16 or wider, within the bound.
A program may use at most 192 MiB of HBM per device.

```python
import math
import jax
import jax.numpy as jnp
from jax import lax

ORDER = 4194304
BLOCK = 128
SLOTS = 32
RHS = 2
ITERS = 2
TILE_ROWS = 4096
TILE_COLS = 8192
N_ROW = 8
N_COL = 4


def tile_numbers():
    return jnp.arange(N_ROW, dtype=jnp.int32)[:, None] * N_COL + jnp.arange(N_COL, dtype=jnp.int32)[None, :]


def pool_draw(key, first, second, range_len):
    inner = jnp.broadcast_to(jnp.arange(range_len - 2, dtype=jnp.int32) + 1, (first, second, range_len - 2))
    mixed = jax.random.permutation(key, inner, axis=2, independent=True).astype(jnp.int32)
    top_value = jnp.full((first, second, 1), range_len - 1, jnp.int32)
    low_value = jnp.zeros((first, second, 1), jnp.int32)
    return jnp.concatenate([top_value, low_value, mixed], axis=2).astype(jnp.int32)


def draw_coords(key, part):
    key_rows, key_cols, key_rpool, key_cpool = jax.random.split(jax.random.fold_in(key, 11), 4)
    range_len = TILE_ROWS // N_COL
    row_cap = SLOTS // N_COL
    col_cap = SLOTS // N_ROW
    slot_base = jnp.broadcast_to(jnp.arange(SLOTS, dtype=jnp.int32), (N_ROW, N_COL, SLOTS))
    row_perm = jax.random.permutation(key_rows, slot_base, axis=2, independent=True).astype(jnp.int32)
    col_perm = jax.random.permutation(key_cols, slot_base, axis=2, independent=True).astype(jnp.int32)
    row_pool = pool_draw(key_rpool, N_ROW, N_COL, range_len)
    col_pool = pool_draw(key_cpool, N_COL, N_ROW, range_len)
    p_index = jnp.arange(N_ROW, dtype=jnp.int32)[:, None, None]
    q_index = jnp.arange(N_COL, dtype=jnp.int32)[None, :, None]
    row_owner = row_perm % N_COL
    row_rank = row_perm // N_COL
    row_pos = (q_index * row_cap + row_rank) % range_len
    block_rows = row_owner * range_len + row_pool[p_index, row_owner, row_pos]
    col_owner = col_perm % N_ROW
    col_rank = col_perm // N_ROW
    col_pos = (p_index * col_cap + col_rank) % range_len
    block_cols = col_owner * range_len + col_pool[q_index, col_owner, col_pos]
    return jnp.stack([block_rows, block_cols], axis=-1).astype(jnp.int32)


def draw_counts(key, part):
    key_base, key_pick = jax.random.split(jax.random.fold_in(key, 23))
    used = SLOTS - jax.random.randint(key_base, (N_ROW, N_COL), 0, SLOTS // 2 + 1, dtype=jnp.int32)
    picks = jax.random.permutation(key_pick, N_ROW * N_COL)[:2].astype(jnp.int32)
    numbers = tile_numbers()
    used = jnp.where(numbers == picks[0], SLOTS, jnp.where(numbers == picks[1], SLOTS - SLOTS // 2, used))
    return used.astype(jnp.int32)


def draw_rhs(key, part):
    key_base, key_scale = jax.random.split(jax.random.fold_in(key, 37))
    scales = jnp.exp(jax.random.uniform(key_scale, (RHS, ORDER), jnp.float32) * math.log(10.0))
    base = jnp.clip(jax.random.normal(key_base, (RHS, ORDER), jnp.float32), -5.0, 5.0)
    return (base * scales).astype(jnp.float32)


def level_of(own_key, extent, cuts, smallest, largest):
    level, own = 1.0, jax.random.fold_in(own_key, 6)
    for dim, shards_of in cuts:
        heights = jnp.exp(jax.random.uniform(jax.random.fold_in(own, dim), (shards_of,), jnp.float32, smallest / len(cuts), largest / len(cuts)))
        level = level * jnp.repeat(heights, extent[dim] // shards_of).reshape([-1 if axis == dim else 1 for axis in range(len(extent))])
    return level


def gaussian(stream_key, dims, scale, reach, pieces=(), held_as=jnp.bfloat16):
    values = jax.random.normal(stream_key, dims, jnp.float32) * scale
    if len(pieces) > 0:
        values = level_of(stream_key, dims, pieces, -0.22, 0.18) * values
    return jnp.clip(values, min=-reach, max=reach).astype(held_as)


def setup_inputs(seed: int = 0) -> dict:
    arg_keys = jax.random.split(jax.random.key(seed), 5)
    return {
        "tiles": gaussian(arg_keys[0], (N_ROW, N_COL, SLOTS, BLOCK, BLOCK), (2 * BLOCK) ** -0.5, 0.375, ((0, 8), (1, 4))),
        "coords": draw_coords(jax.random.fold_in(arg_keys[4], 71), 0),
        "counts": draw_counts(jax.random.fold_in(arg_keys[4], 71), 0),
        "rhs": draw_rhs(jax.random.fold_in(arg_keys[4], 71), 0),
    }


EPS = 1e-06

def rounded(values):
    return lax.optimization_barrier(values.astype(jnp.bfloat16))

def norm_of(vector_bf):
    values = vector_bf.astype(jnp.float32)
    return jnp.sqrt(lax.optimization_barrier(jnp.sum(values * values, axis=1)) + EPS)

def tile_forward(tile_data, slot_coords, count, segment):
    valid = (jnp.arange(SLOTS) < count).astype(jnp.float32)
    blocks = segment.reshape(RHS, TILE_COLS, BLOCK).astype(jnp.float32)
    picked = jnp.take(blocks, slot_coords[:, 1], axis=1)
    products = jnp.einsum('rkc,kdc->krd', picked, tile_data.astype(jnp.float32), precision=lax.Precision.HIGHEST)
    products = products * valid[:, None, None]
    summed = jax.ops.segment_sum(products, slot_coords[:, 0], num_segments=TILE_ROWS)
    partial_sum = jnp.transpose(summed, (1, 0, 2)).reshape(RHS, TILE_ROWS * BLOCK)
    return rounded(partial_sum).astype(jnp.float32)

def tile_adjoint(tile_data, slot_coords, count, segment):
    valid = (jnp.arange(SLOTS) < count).astype(jnp.float32)
    blocks = segment.reshape(RHS, TILE_ROWS, BLOCK).astype(jnp.float32)
    picked = jnp.take(blocks, slot_coords[:, 0], axis=1)
    products = jnp.einsum('rkd,kdc->krc', picked, tile_data.astype(jnp.float32), precision=lax.Precision.HIGHEST)
    products = products * valid[:, None, None]
    summed = jax.ops.segment_sum(products, slot_coords[:, 1], num_segments=TILE_COLS)
    partial_sum = jnp.transpose(summed, (1, 0, 2)).reshape(RHS, TILE_COLS * BLOCK)
    return rounded(partial_sum).astype(jnp.float32)

def apply_forward(tiles, coords, counts, vector_bf):
    segments = vector_bf.reshape(RHS, N_COL, TILE_COLS * BLOCK)

    def one_row(row_index):

        def add_tile(total, col_index):
            term = tile_forward(tiles[row_index, col_index], coords[row_index, col_index], counts[row_index, col_index], segments[:, col_index])
            return (total + term, None)
        total, _ = lax.scan(add_tile, jnp.zeros((RHS, TILE_ROWS * BLOCK), jnp.float32), jnp.arange(N_COL))
        return total
    stacked = lax.map(one_row, jnp.arange(N_ROW))
    return jnp.transpose(stacked, (1, 0, 2)).reshape(RHS, ORDER)

def apply_adjoint(tiles, coords, counts, vector_bf):
    segments = vector_bf.reshape(RHS, N_ROW, TILE_ROWS * BLOCK)

    def one_col(col_index):

        def add_tile(total, row_index):
            term = tile_adjoint(tiles[row_index, col_index], coords[row_index, col_index], counts[row_index, col_index], segments[:, row_index])
            return (total + term, None)
        total, _ = lax.scan(add_tile, jnp.zeros((RHS, TILE_COLS * BLOCK), jnp.float32), jnp.arange(N_ROW))
        return total
    stacked = lax.map(one_col, jnp.arange(N_COL))
    return jnp.transpose(stacked, (1, 0, 2)).reshape(RHS, ORDER)

def reference(tiles, coords, counts, rhs):
    u_rounded = rounded(rhs)
    beta_now = norm_of(u_rounded)
    u_unit = u_rounded.astype(jnp.float32) / beta_now[:, None]
    v_rounded = rounded(apply_adjoint(tiles, coords, counts, u_rounded) / beta_now[:, None])
    alpha_now = norm_of(v_rounded)
    v_unit = v_rounded.astype(jnp.float32) / alpha_now[:, None]
    direction = v_unit
    solution = jnp.zeros((RHS, ORDER), jnp.float32)
    phi_bar = beta_now
    rho_bar = alpha_now
    for step in range(ITERS):
        forward = apply_forward(tiles, coords, counts, v_rounded)
        u_rounded = rounded(forward / alpha_now[:, None] - alpha_now[:, None] * u_unit)
        beta_now = norm_of(u_rounded)
        rho_value = jnp.sqrt(rho_bar * rho_bar + beta_now * beta_now)
        cosine = rho_bar / rho_value
        sine = beta_now / rho_value
        phi_value = cosine * phi_bar
        phi_bar = sine * phi_bar
        solution = solution + (phi_value / rho_value)[:, None] * direction
        u_unit = u_rounded.astype(jnp.float32) / beta_now[:, None]
        if step + 1 < ITERS:
            adjoint = apply_adjoint(tiles, coords, counts, u_rounded)
            v_rounded = rounded(adjoint / beta_now[:, None] - beta_now[:, None] * v_unit)
            alpha_now = norm_of(v_rounded)
            theta_value = sine * alpha_now
            rho_bar = -cosine * alpha_now
            v_unit = v_rounded.astype(jnp.float32) / alpha_now[:, None]
            direction = v_unit - (theta_value / rho_value)[:, None] * direction
    return (solution, phi_bar)
```

```python
import functools

import jax
import jax.numpy as jnp
from jax import lax
from jax.experimental import pallas as pl
from jax.experimental.pallas import tpu as pltpu
from jax.sharding import PartitionSpec as P

EPS = 1e-06
LANES = 128
BF = jnp.bfloat16
F32 = jnp.float32


def iota(shape, dim):
    return lax.broadcasted_iota(jnp.int32, shape, dim)


def diagonal_dot(values, stacked, slots):
    row_slot = iota(values.shape, 0) % slots
    wide = jnp.concatenate(
        [jnp.where(row_slot == k, values, 0.0).astype(BF) for k in range(slots)], axis=1
    )
    return jnp.dot(wide, stacked, preferred_element_type=F32)


def per_realization(products, rows):
    total = jnp.sum(products.reshape(-1, rows, LANES), axis=0)
    half = rows // 2
    lanes = [jnp.sum(total[r * half : (r + 1) * half], axis=0, keepdims=True) for r in range(2)]
    return [jnp.sum(lane, axis=1, keepdims=True) for lane in lanes]


def solver(
    nr, nc, slots, range_len,
    coords, counts, tiles_hbm, rhs_hbm,
    out_ref, phi_ref,
    rhs_v, ub, tiles_v, tt, row_ids, col_ids, picks_out, picks_in, c0, c1, d0, d1,
    stats_col, stats_row, m_col, m_full, sub_full, place,
    load_sem, send_col, recv_col, send_row, recv_row,
):
    me_p = lax.axis_index("row")
    me_q = lax.axis_index("col")
    rows = 2 * slots
    per = LANES // slots

    load_rhs = pltpu.make_async_copy(rhs_hbm, rhs_v, load_sem.at[0])
    load_tiles = pltpu.make_async_copy(tiles_hbm, tiles_v, load_sem.at[1])
    load_rhs.start()
    load_tiles.start()

    def row_peer(o):
        return (lax.rem(me_p + o, nr), me_q)

    def col_peer(o):
        return (me_p, lax.rem(me_q + o, nc))

    barrier = pltpu.get_barrier_semaphore()
    for o in range(1, nr):
        pl.semaphore_signal(
            barrier, inc=1, device_id=row_peer(o), device_id_type=pl.DeviceIdType.MESH
        )
    for o in range(1, nc):
        pl.semaphore_signal(
            barrier, inc=1, device_id=col_peer(o), device_id_type=pl.DeviceIdType.MESH
        )

    lane = iota((8, LANES), 1)
    lane_slot = lane % slots
    used = counts[0, 0]
    row_lane = jnp.full((8, LANES), -1, jnp.int32)
    col_lane = jnp.full((8, LANES), -1, jnp.int32)
    for k in range(slots):
        here = (lane_slot == k) & (k < used)
        row_lane = jnp.where(here, coords[0, 0, k, 0], row_lane)
        col_lane = jnp.where(here, coords[0, 0, k, 1], col_lane)
    row_ids[me_q] = row_lane.astype(F32)
    col_ids[me_p] = col_lane.astype(F32)

    pl.semaphore_wait(barrier, nr + nc - 2)

    sent = []

    def send_over_col(phase, source, target):
        copies = []
        for o in range(1, nc):
            copy = pltpu.make_async_remote_copy(
                src_ref=source(lax.rem(me_q + o, nc)),
                dst_ref=target.at[me_q],
                send_sem=send_col.at[phase, o - 1],
                recv_sem=recv_col.at[phase, o - 1],
                device_id=col_peer(o),
                device_id_type=pl.DeviceIdType.MESH,
            )
            copy.start()
            copies.append(copy)
        sent.extend(copies)
        return copies

    def send_over_row(phase, buffer):
        copies = []
        for o in range(1, nr):
            copy = pltpu.make_async_remote_copy(
                src_ref=buffer.at[me_p],
                dst_ref=buffer.at[me_p],
                send_sem=send_row.at[phase, o - 1],
                recv_sem=recv_row.at[phase, o - 1],
                device_id=row_peer(o),
                device_id_type=pl.DeviceIdType.MESH,
            )
            copy.start()
            copies.append(copy)
        sent.extend(copies)
        return copies

    def arrived(copies):
        for copy in copies:
            copy.wait_recv()

    row_ids_copies = send_over_col(0, lambda peer: row_ids.at[me_q], row_ids)
    col_ids_copies = send_over_row(0, col_ids)

    load_rhs.wait()
    squares = []
    for r in range(2):
        part = rhs_v[pl.ds(r, range_len, stride=2), :].astype(BF)
        ub[:, r * LANES : (r + 1) * LANES] = part
        values = part.astype(F32)
        line = jnp.sum(values * values, axis=0, keepdims=True)
        squares.append(jnp.sum(line, axis=1, keepdims=True))

    arrived(row_ids_copies)
    width = min(LANES, range_len)
    base = (me_q * range_len).astype(F32)
    for g in range(nc // per):
        ids = row_ids[g * per]
        for j in range(1, per):
            ids = jnp.where(lane // slots == j, row_ids[g * per + j], ids)
        local = jnp.broadcast_to(ids[0:1] - base, (LANES, LANES)).T[:, :width]
        column = iota((LANES, width), 1).astype(F32)
        onehot = jnp.concatenate(
            [
                jnp.where(local == column + float(c * width), 1.0, 0.0).astype(BF)
                for c in range(range_len // width)
            ],
            axis=1,
        )
        taken = jnp.dot(onehot, ub[...], preferred_element_type=F32).astype(BF)
        for j in range(per):
            for r in range(2):
                picks_out[g * per + j, r * slots : (r + 1) * slots, :] = taken[
                    j * slots : (j + 1) * slots, r * LANES : (r + 1) * LANES
                ]
    picks_copies = send_over_col(1, lambda peer: picks_out.at[peer], picks_in)
    picks_in[me_q] = picks_out[me_q]

    half_lane = lane // rows
    lane_r = ((lane // slots) % 2).astype(F32)

    def coded(first, second):
        return 2.0 * jnp.where(half_lane == 0, first, second) + lane_r

    def upright(code):
        return jnp.broadcast_to(code[0:1], (LANES, LANES)).T

    row_codes = [coded(row_ids[2 * s], row_ids[2 * s + 1]) for s in range(nc // 2)]
    for s in range(nc // 2):
        sub = upright(row_codes[s])
        sub_full[s * LANES : (s + 1) * LANES, :] = sub
        for t in range(nc // 2):
            code = row_codes[t][0:1]
            m_full[s * LANES : (s + 1) * LANES, t * LANES : (t + 1) * LANES] = jnp.where(
                (sub == code) & (code >= 0.0), 1.0, 0.0
            ).astype(BF)
    load_tiles.wait()
    block = tiles_v.shape[1]

    arrived(picks_copies)
    u0 = picks_in[0].astype(F32)
    for j in range(1, nc):
        u0 = u0 + picks_in[j].astype(F32)

    stacked = tiles_v[...].reshape(slots * block, block)
    c0_own = diagonal_dot(u0, stacked, slots).astype(BF)
    c0[me_p] = c0_own
    c0_copies = send_over_row(1, c0)

    arrived(col_ids_copies)
    sub_col = upright(coded(col_ids[me_p], col_ids[me_p]))[:rows]
    col_base = (me_p * (2 * range_len)).astype(F32)
    chunk = min(256, 2 * range_len)
    for s in range(nr // 2):
        code = coded(col_ids[2 * s], col_ids[2 * s + 1])[0:1]
        m_col[:, s * LANES : (s + 1) * LANES] = jnp.where(
            (sub_col == code) & (code >= 0.0), 1.0, 0.0
        ).astype(BF)
    for k in range(slots):
        tt[k * block : (k + 1) * block, :] = tiles_v[k].astype(F32).T.astype(BF)

    col_live = sub_col >= 0.0
    own_rows = pl.ds(pl.multiple_of(me_q * rows, rows), rows)
    m_row = m_full[own_rows, :]
    row_live = sub_full[own_rows, :] >= 0.0

    def total_col(buffer):
        return jnp.dot(
            m_col[...], buffer[...].reshape(nr * rows, LANES), preferred_element_type=F32
        )

    def total_row(matches, buffer):
        return jnp.dot(
            matches, buffer[...].reshape(nc * rows, LANES), preferred_element_type=F32
        )

    def inner(own, total, live):
        return per_realization(jnp.where(live, own.astype(F32) * total, 0.0), rows)

    arrived(c0_copies)
    g0 = total_col(c0)
    d0_own = diagonal_dot(g0, tt[...], slots).astype(BF)
    d0[me_q] = d0_own
    d0_copies = send_over_col(2, lambda peer: d0.at[me_q], d0)
    gg = inner(c0_own, g0, col_live)

    @pl.loop(0, 2 * range_len // chunk)
    def _(i):
        start = pl.multiple_of(i * chunk, chunk)
        row_number = iota((chunk, LANES), 0).astype(F32) + start.astype(F32)
        for s in range(nr // 2):
            code = coded(col_ids[2 * s], col_ids[2 * s + 1])[0:1]
            place[pl.ds(start, chunk), s * LANES : (s + 1) * LANES] = jnp.where(
                row_number == code - col_base, 1.0, 0.0
            ).astype(BF)

    arrived(d0_copies)
    f0 = total_row(m_row, d0)
    c1_own = diagonal_dot(f0, stacked, slots).astype(BF)
    c1[me_p] = c1_own
    c1_copies = send_over_row(2, c1)
    ff = inner(d0_own, f0, row_live)

    arrived(c1_copies)
    g1 = total_col(c1)
    d1_own = diagonal_dot(g1, tt[...], slots).astype(BF)
    d1[me_q] = d1_own
    d1_copies = send_over_col(3, lambda peer: d1.at[me_q], d1)
    hh = inner(c1_own, g1, col_live)

    stat_row = iota((16, LANES), 0)
    stats = jnp.zeros((16, LANES), F32)
    for s, pair in enumerate((squares, gg, ff, hh)):
        for r in range(2):
            stats = jnp.where(stat_row == 2 * s + r, pair[r], stats)
    stats_col[me_q] = stats
    stats_col_copies = send_over_col(4, lambda peer: stats_col.at[me_q], stats_col)

    arrived(d1_copies)
    f1 = total_row(m_full[...], d1)
    ee = per_realization(
        jnp.where(
            sub_full[...] >= 0.0, d1[...].reshape(nc * rows, LANES).astype(F32) * f1, 0.0
        ),
        rows,
    )
    arrived(stats_col_copies)
    group = jnp.sum(stats_col[...], axis=0)
    for r in range(2):
        group = jnp.where(stat_row == 8 + r, ee[r], group)
    stats_row[me_p] = group
    stats_row_copies = send_over_row(3, stats_row)
    arrived(stats_row_copies)
    whole = jnp.sum(stats_row[...], axis=0)

    uu, gg, ff, hh, ee = [whole[2 * s : 2 * s + 2] for s in range(5)]

    def norm(square):
        return jnp.sqrt(jnp.maximum(square, 0.0) + EPS)

    beta0 = norm(uu)
    alpha0 = norm(gg / (beta0 * beta0))
    a = 1.0 / (beta0 * alpha0)
    b = alpha0 / beta0
    beta1 = norm(a * a * ff - 2.0 * (a * b) * gg + b * b * uu)
    rho0 = jnp.sqrt(alpha0 * alpha0 + beta1 * beta1)
    cosine = alpha0 / rho0
    sine = beta1 / rho0
    phi0 = cosine * beta0
    phi_bar = sine * beta0
    x = a / beta1
    y = -(b / beta1 + beta1 * a)
    alpha1 = norm(x * x * hh + 2.0 * (x * y) * ff + y * y * gg)
    theta = sine * alpha1
    rho_bar = -cosine * alpha1
    e = x / alpha1
    h = y / alpha1 - (alpha1 / beta1) * a
    w = (alpha1 / beta1) * b
    beta2 = norm(
        e * e * ee + h * h * ff + w * w * uu
        + 2.0 * (e * h) * hh + 2.0 * (e * w) * ff + 2.0 * (h * w) * gg
    )
    rho1 = jnp.sqrt(rho_bar * rho_bar + beta2 * beta2)
    phi1 = (rho_bar / rho1) * phi_bar
    phi_ref[0:2, :] = (beta2 / rho1) * phi_bar
    on_g1 = (phi1 / rho1) * e
    on_g0 = (phi0 / rho0) * a + (phi1 / rho1) * (y / alpha1 - (theta / rho0) * a)

    first = iota((rows, LANES), 0) < slots
    scale0 = jnp.where(first, on_g0[0:1], on_g0[1:2])
    scale1 = jnp.where(first, on_g1[0:1], on_g1[1:2])
    terms = c0[...].astype(F32) * scale0[None] + c1[...].astype(F32) * scale1[None]
    terms = terms.reshape(nr * rows, LANES)
    high = terms.astype(BF)
    low = (terms - high.astype(F32)).astype(BF)
    both = jnp.concatenate([high, low], axis=1)

    @pl.loop(0, 2 * range_len // chunk)
    def _(i):
        here = pl.ds(pl.multiple_of(i * chunk, chunk), chunk)
        placed = jnp.dot(place[here, :], both, preferred_element_type=F32)
        out_ref[here, :] = placed[:, :LANES] + placed[:, LANES:]

    for copy in sent:
        copy.wait_send()


def on_device(nr, nc, tiles, coords, counts, rhs):
    slots, block = tiles.shape[2], tiles.shape[3]
    range_len = rhs.shape[1] // block
    rows = 2 * slots
    piece = rhs.reshape(2, range_len, block).transpose(1, 0, 2).reshape(2 * range_len, block)
    dma = pltpu.SemaphoreType.DMA
    placed, phi = pl.pallas_call(
        functools.partial(solver, nr, nc, slots, range_len),
        out_shape=(
            jax.ShapeDtypeStruct((2 * range_len, block), F32),
            jax.ShapeDtypeStruct((8, LANES), F32),
        ),
        in_specs=[
            pl.BlockSpec(memory_space=pltpu.SMEM),
            pl.BlockSpec(memory_space=pltpu.SMEM),
            pl.BlockSpec(memory_space=pl.ANY),
            pl.BlockSpec(memory_space=pl.ANY),
        ],
        out_specs=(
            pl.BlockSpec(memory_space=pltpu.VMEM),
            pl.BlockSpec(memory_space=pltpu.VMEM),
        ),
        scratch_shapes=[
            pltpu.VMEM((2 * range_len, block), F32),
            pltpu.VMEM((range_len, 2 * block), BF),
            pltpu.VMEM((slots, block, block), BF),
            pltpu.VMEM((slots * block, block), BF),
            pltpu.VMEM((nc, 8, LANES), F32),
            pltpu.VMEM((nr, 8, LANES), F32),
            pltpu.VMEM((nc, rows, block), BF),
            pltpu.VMEM((nc, rows, block), BF),
            pltpu.VMEM((nr, rows, block), BF),
            pltpu.VMEM((nr, rows, block), BF),
            pltpu.VMEM((nc, rows, block), BF),
            pltpu.VMEM((nc, rows, block), BF),
            pltpu.VMEM((nc, 16, LANES), F32),
            pltpu.VMEM((nr, 16, LANES), F32),
            pltpu.VMEM((rows, nr * rows), BF),
            pltpu.VMEM((nc * rows, nc * rows), BF),
            pltpu.VMEM((nc * rows, LANES), F32),
            pltpu.VMEM((2 * range_len, nr * rows), BF),
            dma((2,)),
            dma((5, nc - 1)),
            dma((5, nc - 1)),
            dma((4, nr - 1)),
            dma((4, nr - 1)),
        ],
        compiler_params=pltpu.CompilerParams(
            collective_id=0, has_side_effects=True, vmem_limit_bytes=48 * 1024 * 1024
        ),
    )(coords, counts, tiles[0, 0], piece)
    answer = placed.reshape(range_len, 2, block).transpose(1, 0, 2).reshape(2, range_len * block)
    return answer, phi[:2, 0]


def solution(mesh):
    nr, nc = mesh.shape["row"], mesh.shape["col"]
    return jax.shard_map(
        functools.partial(on_device, nr, nc),
        mesh=mesh,
        in_specs=(
            P("row", "col", None, None, None),
            P("row", "col", None, None),
            P("row", "col"),
            P(None, ("row", "col")),
        ),
        out_specs=(P(None, ("col", "row")), P()),
        check_vma=False,
    )
```

```python
import functools

import jax
import jax.numpy as jnp
from jax import lax
from jax.experimental import pallas as pl
from jax.experimental.pallas import tpu as pltpu
from jax.sharding import PartitionSpec as P

EPS = 1e-06
LANES = 128
BF = jnp.bfloat16
F32 = jnp.float32


def iota(shape, dim):
    return lax.broadcasted_iota(jnp.int32, shape, dim)


def diagonal_dot(values, stacked, slots):
    group = 8
    row_slot = iota((2 * group, LANES), 0) % group
    parts = []
    for start in range(0, slots, group):
        pair = jnp.concatenate(
            [values[r * slots + start : r * slots + start + group] for r in range(2)], axis=0
        )
        wide = jnp.concatenate(
            [jnp.where(row_slot == k, pair, 0.0).astype(BF) for k in range(group)], axis=1
        )
        parts.append(
            jnp.dot(
                wide,
                stacked[start * LANES : (start + group) * LANES],
                preferred_element_type=F32,
            )
        )
    return jnp.concatenate([p[:group] for p in parts] + [p[group:] for p in parts], axis=0)


def per_realization(products, rows):
    total = jnp.sum(products.reshape(-1, rows, LANES), axis=0)
    half = rows // 2
    lanes = [jnp.sum(total[r * half : (r + 1) * half], axis=0, keepdims=True) for r in range(2)]
    return [jnp.sum(lane, axis=1, keepdims=True) for lane in lanes]


def solver(
    nr, nc, slots, range_len,
    coords_hbm, counts, tiles_hbm, rhs_hbm,
    out_ref, phi_ref,
    coords_v, rhs_v, ub, tiles_v, tt, row_ids, col_ids, picks_out, picks_in, c0, c1, d0, d1,
    stats_col, stats_row, m_col, m_full, sub_full, place, placed1,
    load_sem, send_col, recv_col, send_row, recv_row,
):
    me_p = lax.axis_index("row")
    me_q = lax.axis_index("col")
    rows = 2 * slots
    per = LANES // slots

    load_rhs = pltpu.make_async_copy(rhs_hbm, rhs_v, load_sem.at[0])
    load_tiles = pltpu.make_async_copy(tiles_hbm, tiles_v, load_sem.at[1])
    load_coords = pltpu.make_async_copy(coords_hbm, coords_v, load_sem.at[2])
    load_coords.start()
    load_rhs.start()
    load_tiles.start()

    def row_peer(o):
        return (lax.rem(me_p + o, nr), me_q)

    def col_peer(o):
        return (me_p, lax.rem(me_q + o, nc))

    barrier = pltpu.get_barrier_semaphore()
    for o in range(1, nr):
        pl.semaphore_signal(
            barrier, inc=1, device_id=row_peer(o), device_id_type=pl.DeviceIdType.MESH
        )
    for o in range(1, nc):
        pl.semaphore_signal(
            barrier, inc=1, device_id=col_peer(o), device_id_type=pl.DeviceIdType.MESH
        )

    lane = iota((1, LANES), 1)
    load_coords.wait()
    numbers = jnp.concatenate([coords_v[...]] * per, axis=1)
    numbers = jnp.where(iota((2, LANES), 1) % slots < counts[0, 0], numbers, -1).astype(F32)
    row_ids[me_q] = numbers[0:1]
    col_ids[me_p] = numbers[1:2]

    pl.semaphore_wait(barrier, nr + nc - 2)

    sent = []

    def send_over_col(phase, source, target):
        copies = []
        for o in range(1, nc):
            copy = pltpu.make_async_remote_copy(
                src_ref=source(lax.rem(me_q + o, nc)),
                dst_ref=target.at[me_q],
                send_sem=send_col.at[phase, o - 1],
                recv_sem=recv_col.at[phase, o - 1],
                device_id=col_peer(o),
                device_id_type=pl.DeviceIdType.MESH,
            )
            copy.start()
            copies.append(copy)
        sent.extend(copies)
        return copies

    def send_over_row(phase, buffer):
        copies = []
        for o in range(1, nr):
            copy = pltpu.make_async_remote_copy(
                src_ref=buffer.at[me_p],
                dst_ref=buffer.at[me_p],
                send_sem=send_row.at[phase, o - 1],
                recv_sem=recv_row.at[phase, o - 1],
                device_id=row_peer(o),
                device_id_type=pl.DeviceIdType.MESH,
            )
            copy.start()
            copies.append(copy)
        sent.extend(copies)
        return copies

    def arrived(copies):
        for copy in copies:
            copy.wait_recv()

    row_ids_copies = send_over_col(0, lambda peer: row_ids.at[me_q], row_ids)
    col_ids_copies = send_over_row(0, col_ids)

    load_rhs.wait()
    squares = []
    for r in range(2):
        part = rhs_v[pl.ds(r, range_len, stride=2), :].astype(BF)
        ub[:, r * LANES : (r + 1) * LANES] = part
        values = part.astype(F32)
        line = jnp.sum(values * values, axis=0, keepdims=True)
        squares.append(jnp.sum(line, axis=1, keepdims=True))

    arrived(row_ids_copies)
    width = min(LANES, range_len)
    base = (me_q * range_len).astype(F32)
    for g in range(nc // per):
        ids = row_ids[g * per]
        for j in range(1, per):
            ids = jnp.where(lane // slots == j, row_ids[g * per + j], ids)
        local = jnp.broadcast_to(ids - base, (LANES, LANES)).T[:, :width]
        column = iota((LANES, width), 1).astype(F32)
        onehot = jnp.concatenate(
            [
                jnp.where(local == column + float(c * width), 1.0, 0.0).astype(BF)
                for c in range(range_len // width)
            ],
            axis=1,
        )
        taken = jnp.dot(onehot, ub[...], preferred_element_type=F32).astype(BF)
        for j in range(per):
            for r in range(2):
                picks_out[g * per + j, r * slots : (r + 1) * slots, :] = taken[
                    j * slots : (j + 1) * slots, r * LANES : (r + 1) * LANES
                ]
    picks_copies = send_over_col(1, lambda peer: picks_out.at[peer], picks_in)
    picks_in[me_q] = picks_out[me_q]

    half_lane = lane // rows
    lane_r = ((lane // slots) % 2).astype(F32)

    def coded(first, second):
        return 2.0 * jnp.where(half_lane == 0, first, second) + lane_r

    def upright(code):
        return jnp.broadcast_to(code, (LANES, LANES)).T

    row_codes = [coded(row_ids[2 * s], row_ids[2 * s + 1]) for s in range(nc // 2)]
    for s in range(nc // 2):
        sub = upright(row_codes[s])
        sub_full[s * LANES : (s + 1) * LANES, :] = sub
        for t in range(nc // 2):
            code = row_codes[t]
            m_full[s * LANES : (s + 1) * LANES, t * LANES : (t + 1) * LANES] = jnp.where(
                (sub == code) & (code >= 0.0), 1.0, 0.0
            ).astype(BF)
    load_tiles.wait()
    block = tiles_v.shape[1]

    def turn(first, last):
        for k in range(first, last):
            tt[k * block : (k + 1) * block, :] = tiles_v[k].astype(F32).T.astype(BF)

    turn(0, slots // 2)

    arrived(picks_copies)
    u0 = picks_in[0].astype(F32)
    for j in range(1, nc):
        u0 = u0 + picks_in[j].astype(F32)

    stacked = tiles_v[...].reshape(slots * block, block)
    c0_own = diagonal_dot(u0, stacked, slots).astype(BF)
    c0[me_p] = c0_own
    c0_copies = send_over_row(1, c0)

    arrived(col_ids_copies)
    sub_col = upright(coded(col_ids[me_p], col_ids[me_p]))[:rows]
    col_base = (me_p * (2 * range_len)).astype(F32)
    chunk = min(256, 2 * range_len)
    for s in range(nr // 2):
        code = coded(col_ids[2 * s], col_ids[2 * s + 1])
        m_col[:, s * LANES : (s + 1) * LANES] = jnp.where(
            (sub_col == code) & (code >= 0.0), 1.0, 0.0
        ).astype(BF)
    turn(slots // 2, slots)

    col_live = sub_col >= 0.0
    own_rows = pl.ds(pl.multiple_of(me_q * rows, rows), rows)
    m_row = m_full[own_rows, :]
    row_live = sub_full[own_rows, :] >= 0.0

    def total_col(buffer):
        return jnp.dot(
            m_col[...], buffer[...].reshape(nr * rows, LANES), preferred_element_type=F32
        )

    def total_row(matches, buffer):
        return jnp.dot(
            matches, buffer[...].reshape(nc * rows, LANES), preferred_element_type=F32
        )

    def inner(own, total, live):
        return per_realization(jnp.where(live, own.astype(F32) * total, 0.0), rows)

    @pl.loop(0, 2 * range_len // chunk)
    def _(i):
        start = pl.multiple_of(i * chunk, chunk)
        row_number = iota((chunk, LANES), 0).astype(F32) + start.astype(F32)
        for s in range(nr // 2):
            code = coded(col_ids[2 * s], col_ids[2 * s + 1])
            place[pl.ds(start, chunk), s * LANES : (s + 1) * LANES] = jnp.where(
                row_number == code - col_base, 1.0, 0.0
            ).astype(BF)

    arrived(c0_copies)
    g0 = total_col(c0)
    d0_own = diagonal_dot(g0, tt[...], slots).astype(BF)
    d0[me_q] = d0_own
    d0_copies = send_over_col(2, lambda peer: d0.at[me_q], d0)
    gg = inner(c0_own, g0, col_live)

    arrived(d0_copies)
    f0 = total_row(m_row, d0)
    c1_own = diagonal_dot(f0, stacked, slots).astype(BF)
    c1[me_p] = c1_own
    c1_copies = send_over_row(2, c1)
    ff = inner(d0_own, f0, row_live)

    def put(buffer, target):
        flat = buffer[...].reshape(nr * rows, LANES)

        @pl.loop(0, 2 * range_len // chunk)
        def _(i):
            here = pl.ds(pl.multiple_of(i * chunk, chunk), chunk)
            target[here, :] = jnp.dot(place[here, :], flat, preferred_element_type=F32)

    put(c0, out_ref)
    arrived(c1_copies)
    g1 = total_col(c1)
    d1_own = diagonal_dot(g1, tt[...], slots).astype(BF)
    d1[me_q] = d1_own
    d1_copies = send_over_col(3, lambda peer: d1.at[me_q], d1)
    hh = inner(c1_own, g1, col_live)

    stats = jnp.zeros((1, LANES), F32)
    for s, pair in enumerate((squares, gg, ff, hh)):
        for r in range(2):
            stats = jnp.where(lane == 2 * s + r, pair[r], stats)
    stats_col[me_q] = stats
    stats_col_copies = send_over_col(4, lambda peer: stats_col.at[me_q], stats_col)

    put(c1, placed1)
    arrived(d1_copies)
    f1 = total_row(m_full[...], d1)
    ee = per_realization(
        jnp.where(
            sub_full[...] >= 0.0, d1[...].reshape(nc * rows, LANES).astype(F32) * f1, 0.0
        ),
        rows,
    )
    arrived(stats_col_copies)
    group = jnp.sum(stats_col[...], axis=0)
    for r in range(2):
        group = jnp.where(lane == 8 + r, ee[r], group)
    stats_row[me_p] = group
    stats_row_copies = send_over_row(3, stats_row)
    arrived(stats_row_copies)
    whole = jnp.sum(stats_row[...], axis=0)

    uu, gg, ff, hh, ee = [whole] + [pltpu.roll(whole, LANES - 2 * s, 1) for s in range(1, 5)]

    def norm(square):
        return jnp.sqrt(jnp.maximum(square, 0.0) + EPS)

    beta0 = norm(uu)
    alpha0 = norm(gg / (beta0 * beta0))
    a = 1.0 / (beta0 * alpha0)
    b = alpha0 / beta0
    beta1 = norm(a * a * ff - 2.0 * (a * b) * gg + b * b * uu)
    rho0 = jnp.sqrt(alpha0 * alpha0 + beta1 * beta1)
    cosine = alpha0 / rho0
    sine = beta1 / rho0
    phi0 = cosine * beta0
    phi_bar = sine * beta0
    x = a / beta1
    y = -(b / beta1 + beta1 * a)
    alpha1 = norm(x * x * hh + 2.0 * (x * y) * ff + y * y * gg)
    theta = sine * alpha1
    rho_bar = -cosine * alpha1
    e = x / alpha1
    h = y / alpha1 - (alpha1 / beta1) * a
    w = (alpha1 / beta1) * b
    beta2 = norm(
        e * e * ee + h * h * ff + w * w * uu
        + 2.0 * (e * h) * hh + 2.0 * (e * w) * ff + 2.0 * (h * w) * gg
    )
    rho1 = jnp.sqrt(rho_bar * rho_bar + beta2 * beta2)
    phi1 = (rho_bar / rho1) * phi_bar
    phi_ref[...] = ((beta2 / rho1) * phi_bar)[:, 0:2]
    on_g1 = (phi1 / rho1) * e
    on_g0 = (phi0 / rho0) * a + (phi1 / rho1) * (y / alpha1 - (theta / rho0) * a)

    even = iota((chunk, LANES), 0) % 2 == 0
    scale0 = jnp.where(even, on_g0[:, 0:1], on_g0[:, 1:2])
    scale1 = jnp.where(even, on_g1[:, 0:1], on_g1[:, 1:2])

    @pl.loop(0, 2 * range_len // chunk)
    def _(i):
        here = pl.ds(pl.multiple_of(i * chunk, chunk), chunk)
        out_ref[here, :] = out_ref[here, :] * scale0 + placed1[here, :] * scale1

    for copy in sent:
        copy.wait_send()


def on_device(nr, nc, tiles, coords, counts, rhs):
    slots, block = tiles.shape[2], tiles.shape[3]
    range_len = rhs.shape[1] // block
    rows = 2 * slots
    piece = rhs.reshape(2, range_len, block).transpose(1, 0, 2).reshape(2 * range_len, block)
    dma = pltpu.SemaphoreType.DMA
    placed, phi = pl.pallas_call(
        functools.partial(solver, nr, nc, slots, range_len),
        out_shape=(
            jax.ShapeDtypeStruct((2 * range_len, block), F32),
            jax.ShapeDtypeStruct((1, 2), F32),
        ),
        in_specs=[
            pl.BlockSpec(memory_space=pltpu.HBM),
            pl.BlockSpec(memory_space=pltpu.SMEM),
            pl.BlockSpec(memory_space=pltpu.HBM),
            pl.BlockSpec(memory_space=pltpu.HBM),
        ],
        out_specs=(
            pl.BlockSpec(memory_space=pltpu.VMEM),
            pl.BlockSpec(memory_space=pltpu.VMEM),
        ),
        scratch_shapes=[
            pltpu.VMEM((2, slots), jnp.int32),
            pltpu.VMEM((2 * range_len, block), F32),
            pltpu.VMEM((range_len, 2 * block), BF),
            pltpu.VMEM((slots, block, block), BF),
            pltpu.VMEM((slots * block, block), BF),
            pltpu.VMEM((nc, 1, LANES), F32),
            pltpu.VMEM((nr, 1, LANES), F32),
            pltpu.VMEM((nc, rows, block), BF),
            pltpu.VMEM((nc, rows, block), BF),
            pltpu.VMEM((nr, rows, block), BF),
            pltpu.VMEM((nr, rows, block), BF),
            pltpu.VMEM((nc, rows, block), BF),
            pltpu.VMEM((nc, rows, block), BF),
            pltpu.VMEM((nc, 1, LANES), F32),
            pltpu.VMEM((nr, 1, LANES), F32),
            pltpu.VMEM((rows, nr * rows), BF),
            pltpu.VMEM((nc * rows, nc * rows), BF),
            pltpu.VMEM((nc * rows, LANES), F32),
            pltpu.VMEM((2 * range_len, nr * rows), BF),
            pltpu.VMEM((2 * range_len, block), F32),
            dma((3,)),
            dma((5, nc - 1)),
            dma((5, nc - 1)),
            dma((4, nr - 1)),
            dma((4, nr - 1)),
        ],
        compiler_params=pltpu.CompilerParams(
            collective_id=0, has_side_effects=True, vmem_limit_bytes=48 * 1024 * 1024
        ),
    )(coords[0, 0].T, counts, tiles[0, 0], piece)
    answer = placed.reshape(range_len, 2, block).transpose(1, 0, 2).reshape(2, range_len * block)
    return answer, phi[0]


def solution(mesh):
    nr, nc = mesh.shape["row"], mesh.shape["col"]
    return jax.shard_map(
        functools.partial(on_device, nr, nc),
        mesh=mesh,
        in_specs=(
            P("row", "col", None, None, None),
            P("row", "col", None, None),
            P("row", "col"),
            P(None, ("row", "col")),
        ),
        out_specs=(P(None, ("col", "row")), P()),
        check_vma=False,
    )
```

```python
import functools

import jax
import jax.numpy as jnp
from jax import lax
from jax.experimental import pallas as pl
from jax.experimental.pallas import tpu as pltpu
from jax.sharding import PartitionSpec as P

EPS = 1e-06
LANES = 128
BF = jnp.bfloat16
F32 = jnp.float32


def iota(shape, dim):
    return lax.broadcasted_iota(jnp.int32, shape, dim)


def diagonal_dot(values, stacked, slots):
    group = 8
    row_slot = iota((2 * group, LANES), 0) % group
    parts = []
    for start in range(0, slots, group):
        pair = jnp.concatenate(
            [values[r * slots + start : r * slots + start + group] for r in range(2)], axis=0
        )
        wide = jnp.concatenate(
            [jnp.where(row_slot == k, pair, 0.0).astype(BF) for k in range(group)], axis=1
        )
        parts.append(
            jnp.dot(
                wide,
                stacked[start * LANES : (start + group) * LANES],
                preferred_element_type=F32,
            )
        )
    return jnp.concatenate([p[:group] for p in parts] + [p[group:] for p in parts], axis=0)


def per_realization(products, rows):
    total = jnp.sum(products.reshape(-1, rows, LANES), axis=0)
    half = rows // 2
    lanes = [jnp.sum(total[r * half : (r + 1) * half], axis=0, keepdims=True) for r in range(2)]
    return [jnp.sum(lane, axis=1, keepdims=True) for lane in lanes]


def solver(
    nr, nc, slots, range_len,
    coords_hbm, counts, tiles_hbm, rhs_hbm,
    out_ref, phi_ref,
    coords_v, rhs_v, ub, tiles_v, tt, row_ids, col_ids, picks_out, picks_in, c0, c1, d0, d1,
    stats_col, stats_row, m_col, m_full, sub_full, place, placed1,
    load_sem, send_col, recv_col, send_row, recv_row,
):
    me_p = lax.axis_index("row")
    me_q = lax.axis_index("col")
    rows = 2 * slots
    per = LANES // slots

    load_rhs = pltpu.make_async_copy(rhs_hbm, rhs_v, load_sem.at[0])
    load_tiles = pltpu.make_async_copy(tiles_hbm, tiles_v, load_sem.at[1])
    load_coords = pltpu.make_async_copy(coords_hbm, coords_v, load_sem.at[2])
    load_coords.start()
    load_rhs.start()
    load_tiles.start()

    def row_peer(o):
        return (lax.rem(me_p + o, nr), me_q)

    def col_peer(o):
        return (me_p, lax.rem(me_q + o, nc))

    barrier = pltpu.get_barrier_semaphore()
    for o in range(1, nr):
        pl.semaphore_signal(
            barrier, inc=1, device_id=row_peer(o), device_id_type=pl.DeviceIdType.MESH
        )
    for o in range(1, nc):
        pl.semaphore_signal(
            barrier, inc=1, device_id=col_peer(o), device_id_type=pl.DeviceIdType.MESH
        )

    lane = iota((1, LANES), 1)
    load_coords.wait()
    numbers = jnp.concatenate([coords_v[...]] * per, axis=1)
    numbers = jnp.where(iota((2, LANES), 1) % slots < counts[0, 0], numbers, -1).astype(F32)
    row_ids[me_q] = numbers[0:1]
    col_ids[me_p] = numbers[1:2]

    pl.semaphore_wait(barrier, nr + nc - 2)

    sent = []

    def send_over_col(phase, source, target):
        copies = []
        for o in range(1, nc):
            copy = pltpu.make_async_remote_copy(
                src_ref=source(lax.rem(me_q + o, nc)),
                dst_ref=target.at[me_q],
                send_sem=send_col.at[phase, o - 1],
                recv_sem=recv_col.at[phase, o - 1],
                device_id=col_peer(o),
                device_id_type=pl.DeviceIdType.MESH,
            )
            copy.start()
            copies.append(copy)
        sent.extend(copies)
        return copies

    def send_over_row(phase, buffer):
        copies = []
        for o in range(1, nr):
            copy = pltpu.make_async_remote_copy(
                src_ref=buffer.at[me_p],
                dst_ref=buffer.at[me_p],
                send_sem=send_row.at[phase, o - 1],
                recv_sem=recv_row.at[phase, o - 1],
                device_id=row_peer(o),
                device_id_type=pl.DeviceIdType.MESH,
            )
            copy.start()
            copies.append(copy)
        sent.extend(copies)
        return copies

    def arrived(copies):
        for copy in copies:
            copy.wait_recv()

    row_ids_copies = send_over_col(0, lambda peer: row_ids.at[me_q], row_ids)
    col_ids_copies = send_over_row(0, col_ids)

    load_rhs.wait()
    squares = []
    for r in range(2):
        part = rhs_v[pl.ds(r, range_len, stride=2), :].astype(BF)
        ub[:, r * LANES : (r + 1) * LANES] = part
        values = part.astype(F32)
        line = jnp.sum(values * values, axis=0, keepdims=True)
        squares.append(jnp.sum(line, axis=1, keepdims=True))

    arrived(row_ids_copies)
    width = min(LANES, range_len)
    base = (me_q * range_len).astype(F32)
    for g in range(nc // per):
        ids = row_ids[g * per]
        for j in range(1, per):
            ids = jnp.where(lane // slots == j, row_ids[g * per + j], ids)
        local = jnp.broadcast_to(ids - base, (LANES, LANES)).T[:, :width]
        column = iota((LANES, width), 1).astype(F32)
        onehot = jnp.concatenate(
            [
                jnp.where(local == column + float(c * width), 1.0, 0.0).astype(BF)
                for c in range(range_len // width)
            ],
            axis=1,
        )
        taken = jnp.dot(onehot, ub[...], preferred_element_type=F32).astype(BF)
        for j in range(per):
            for r in range(2):
                picks_out[g * per + j, r * slots : (r + 1) * slots, :] = taken[
                    j * slots : (j + 1) * slots, r * LANES : (r + 1) * LANES
                ]
    picks_copies = send_over_col(1, lambda peer: picks_out.at[peer], picks_in)
    picks_in[me_q] = picks_out[me_q]

    half_lane = lane // rows
    lane_r = ((lane // slots) % 2).astype(F32)

    def coded(first, second):
        return 2.0 * jnp.where(half_lane == 0, first, second) + lane_r

    def upright(code):
        return jnp.broadcast_to(code, (LANES, LANES)).T

    row_codes = [coded(row_ids[2 * s], row_ids[2 * s + 1]) for s in range(nc // 2)]
    for s in range(nc // 2):
        sub = upright(row_codes[s])
        sub_full[s * LANES : (s + 1) * LANES, :] = sub
        for t in range(nc // 2):
            code = row_codes[t]
            m_full[s * LANES : (s + 1) * LANES, t * LANES : (t + 1) * LANES] = jnp.where(
                (sub == code) & (code >= 0.0), 1.0, 0.0
            ).astype(BF)
    load_tiles.wait()
    block = tiles_v.shape[1]

    def turn(first, last):
        for k in range(first, last):
            tt[k * block : (k + 1) * block, :] = tiles_v[k].astype(F32).T.astype(BF)

    turn(0, slots // 2)

    arrived(picks_copies)
    u0 = picks_in[0].astype(F32)
    for j in range(1, nc):
        u0 = u0 + picks_in[j].astype(F32)

    stacked = tiles_v[...].reshape(slots * block, block)
    c0_own = diagonal_dot(u0, stacked, slots).astype(BF)
    c0[me_p] = c0_own
    c0_copies = send_over_row(1, c0)

    arrived(col_ids_copies)
    sub_col = upright(coded(col_ids[me_p], col_ids[me_p]))[:rows]
    col_base = (me_p * (2 * range_len)).astype(F32)
    chunk = min(256, 2 * range_len)
    for s in range(nr // 2):
        code = coded(col_ids[2 * s], col_ids[2 * s + 1])
        m_col[:, s * LANES : (s + 1) * LANES] = jnp.where(
            (sub_col == code) & (code >= 0.0), 1.0, 0.0
        ).astype(BF)
    turn(slots // 2, slots)

    col_live = sub_col >= 0.0
    own_rows = pl.ds(pl.multiple_of(me_q * rows, rows), rows)
    m_row = m_full[own_rows, :]
    row_live = sub_full[own_rows, :] >= 0.0

    def total_col(buffer):
        return jnp.dot(
            m_col[...], buffer[...].reshape(nr * rows, LANES), preferred_element_type=F32
        )

    def total_row(matches, buffer):
        return jnp.dot(
            matches, buffer[...].reshape(nc * rows, LANES), preferred_element_type=F32
        )

    def inner(own, total, live):
        return per_realization(jnp.where(live, own.astype(F32) * total, 0.0), rows)

    @pl.loop(0, 2 * range_len // chunk)
    def _(i):
        start = pl.multiple_of(i * chunk, chunk)
        row_number = iota((chunk, LANES), 0).astype(F32) + start.astype(F32)
        for s in range(nr // 2):
            code = coded(col_ids[2 * s], col_ids[2 * s + 1])
            place[pl.ds(start, chunk), s * LANES : (s + 1) * LANES] = jnp.where(
                row_number == code - col_base, 1.0, 0.0
            ).astype(BF)

    arrived(c0_copies)
    g0 = total_col(c0)
    d0_own = diagonal_dot(g0, tt[...], slots).astype(BF)
    d0[me_q] = d0_own
    d0_copies = send_over_col(2, lambda peer: d0.at[me_q], d0)
    gg = inner(c0_own, g0, col_live)

    arrived(d0_copies)
    f0 = total_row(m_row, d0)
    c1_own = diagonal_dot(f0, stacked, slots).astype(BF)
    c1[me_p] = c1_own
    c1_copies = send_over_row(2, c1)
    ff = inner(d0_own, f0, row_live)

    def put(buffer, target):
        flat = buffer[...].reshape(nr * rows, LANES)

        @pl.loop(0, 2 * range_len // chunk)
        def _(i):
            here = pl.ds(pl.multiple_of(i * chunk, chunk), chunk)
            target[here, :] = jnp.dot(place[here, :], flat, preferred_element_type=F32)

    put(c0, out_ref)
    arrived(c1_copies)
    g1 = total_col(c1)
    d1_own = diagonal_dot(g1, tt[...], slots).astype(BF)
    d1[me_q] = d1_own
    d1_copies = send_over_col(3, lambda peer: d1.at[me_q], d1)
    hh = inner(c1_own, g1, col_live)

    stats = jnp.zeros((1, LANES), F32)
    for s, pair in enumerate((squares, gg, ff, hh)):
        for r in range(2):
            stats = jnp.where(lane == 2 * s + r, pair[r], stats)
    stats_col[me_q] = stats
    stats_col_copies = send_over_col(4, lambda peer: stats_col.at[me_q], stats_col)

    arrived(d1_copies)
    f1 = total_row(m_full[...], d1)
    ee = per_realization(
        jnp.where(
            sub_full[...] >= 0.0, d1[...].reshape(nc * rows, LANES).astype(F32) * f1, 0.0
        ),
        rows,
    )
    arrived(stats_col_copies)
    group = jnp.sum(stats_col[...], axis=0)
    for r in range(2):
        group = jnp.where(lane == 8 + r, ee[r], group)
    stats_row[me_p] = group
    stats_row_copies = send_over_row(3, stats_row)
    put(c1, placed1)
    arrived(stats_row_copies)
    whole = jnp.sum(stats_row[...], axis=0)

    uu, gg, ff, hh, ee = [whole] + [pltpu.roll(whole, LANES - 2 * s, 1) for s in range(1, 5)]

    def norm(square):
        return jnp.sqrt(jnp.maximum(square, 0.0) + EPS)

    beta0 = norm(uu)
    alpha0 = norm(gg / (beta0 * beta0))
    a = 1.0 / (beta0 * alpha0)
    b = alpha0 / beta0
    beta1 = norm(a * a * ff - 2.0 * (a * b) * gg + b * b * uu)
    rho0 = jnp.sqrt(alpha0 * alpha0 + beta1 * beta1)
    cosine = alpha0 / rho0
    sine = beta1 / rho0
    phi0 = cosine * beta0
    phi_bar = sine * beta0
    x = a / beta1
    y = -(b / beta1 + beta1 * a)
    alpha1 = norm(x * x * hh + 2.0 * (x * y) * ff + y * y * gg)
    theta = sine * alpha1
    rho_bar = -cosine * alpha1
    e = x / alpha1
    h = y / alpha1 - (alpha1 / beta1) * a
    w = (alpha1 / beta1) * b
    beta2 = norm(
        e * e * ee + h * h * ff + w * w * uu
        + 2.0 * (e * h) * hh + 2.0 * (e * w) * ff + 2.0 * (h * w) * gg
    )
    rho1 = jnp.sqrt(rho_bar * rho_bar + beta2 * beta2)
    phi1 = (rho_bar / rho1) * phi_bar
    phi_ref[...] = ((beta2 / rho1) * phi_bar)[:, 0:2]
    on_g1 = (phi1 / rho1) * e
    on_g0 = (phi0 / rho0) * a + (phi1 / rho1) * (y / alpha1 - (theta / rho0) * a)

    even = iota((chunk, LANES), 0) % 2 == 0
    scale0 = jnp.where(even, on_g0[:, 0:1], on_g0[:, 1:2])
    scale1 = jnp.where(even, on_g1[:, 0:1], on_g1[:, 1:2])

    @pl.loop(0, 2 * range_len // chunk)
    def _(i):
        here = pl.ds(pl.multiple_of(i * chunk, chunk), chunk)
        out_ref[here, :] = out_ref[here, :] * scale0 + placed1[here, :] * scale1

    for copy in sent:
        copy.wait_send()


def on_device(nr, nc, tiles, coords, counts, rhs):
    slots, block = tiles.shape[2], tiles.shape[3]
    range_len = rhs.shape[1] // block
    rows = 2 * slots
    piece = rhs.reshape(2, range_len, block).transpose(1, 0, 2).reshape(2 * range_len, block)
    dma = pltpu.SemaphoreType.DMA
    placed, phi = pl.pallas_call(
        functools.partial(solver, nr, nc, slots, range_len),
        out_shape=(
            jax.ShapeDtypeStruct((2 * range_len, block), F32),
            jax.ShapeDtypeStruct((1, 2), F32),
        ),
        in_specs=[
            pl.BlockSpec(memory_space=pltpu.HBM),
            pl.BlockSpec(memory_space=pltpu.SMEM),
            pl.BlockSpec(memory_space=pltpu.HBM),
            pl.BlockSpec(memory_space=pltpu.HBM),
        ],
        out_specs=(
            pl.BlockSpec(memory_space=pltpu.VMEM),
            pl.BlockSpec(memory_space=pltpu.VMEM),
        ),
        scratch_shapes=[
            pltpu.VMEM((2, slots), jnp.int32),
            pltpu.VMEM((2 * range_len, block), F32),
            pltpu.VMEM((range_len, 2 * block), BF),
            pltpu.VMEM((slots, block, block), BF),
            pltpu.VMEM((slots * block, block), BF),
            pltpu.VMEM((nc, 1, LANES), F32),
            pltpu.VMEM((nr, 1, LANES), F32),
            pltpu.VMEM((nc, rows, block), BF),
            pltpu.VMEM((nc, rows, block), BF),
            pltpu.VMEM((nr, rows, block), BF),
            pltpu.VMEM((nr, rows, block), BF),
            pltpu.VMEM((nc, rows, block), BF),
            pltpu.VMEM((nc, rows, block), BF),
            pltpu.VMEM((nc, 1, LANES), F32),
            pltpu.VMEM((nr, 1, LANES), F32),
            pltpu.VMEM((rows, nr * rows), BF),
            pltpu.VMEM((nc * rows, nc * rows), BF),
            pltpu.VMEM((nc * rows, LANES), F32),
            pltpu.VMEM((2 * range_len, nr * rows), BF),
            pltpu.VMEM((2 * range_len, block), F32),
            dma((3,)),
            dma((5, nc - 1)),
            dma((5, nc - 1)),
            dma((4, nr - 1)),
            dma((4, nr - 1)),
        ],
        compiler_params=pltpu.CompilerParams(
            collective_id=0, has_side_effects=True, vmem_limit_bytes=48 * 1024 * 1024
        ),
    )(
        pltpu.with_memory_space_constraint(coords[0, 0].T, pltpu.HBM),
        counts,
        pltpu.with_memory_space_constraint(tiles[0, 0], pltpu.HBM),
        pltpu.with_memory_space_constraint(piece, pltpu.HBM),
    )
    answer = placed.reshape(range_len, 2, block).transpose(1, 0, 2).reshape(2, range_len * block)
    return answer, phi[0]


def solution(mesh):
    nr, nc = mesh.shape["row"], mesh.shape["col"]
    return jax.shard_map(
        functools.partial(on_device, nr, nc),
        mesh=mesh,
        in_specs=(
            P("row", "col", None, None, None),
            P("row", "col", None, None),
            P("row", "col"),
            P(None, ("row", "col")),
        ),
        out_specs=(P(None, ("col", "row")), P()),
        check_vma=False,
    )
```

```python
import functools

import jax
import jax.numpy as jnp
from jax import lax
from jax.experimental import pallas as pl
from jax.experimental.pallas import tpu as pltpu
from jax.sharding import PartitionSpec as P

EPS = 1e-06
LANES = 128
BF = jnp.bfloat16
F32 = jnp.float32


def iota(shape, dim):
    return lax.broadcasted_iota(jnp.int32, shape, dim)


def diagonal_dot(values, stacked, slots):
    group, half = 8, slots // 2
    row_slot = iota((2 * group, LANES), 0) % group
    first, second = [], []
    for start in range(0, half, group):
        pair = jnp.concatenate(
            [values[start : start + group], values[half + start : half + start + group]], axis=0
        )
        wide = jnp.concatenate(
            [jnp.where(row_slot == k, pair, 0.0).astype(BF) for k in range(group)], axis=1
        )
        result = jnp.dot(
            wide,
            stacked[start * LANES : (start + group) * LANES],
            preferred_element_type=F32,
        )
        first.append(result[:group, :LANES])
        second.append(result[group:, LANES:])
    return jnp.concatenate(first + second, axis=0)


def total_of(products):
    line = jnp.sum(products, axis=0, keepdims=True)
    return jnp.sum(line, axis=1, keepdims=True)


def solver(
    nr, nc, slots, range_len,
    coords_hbm, counts, tiles_hbm, rhs_hbm,
    out_ref, phi_ref,
    coords_v, rhs_v, ub, tiles_v, tt, row_ids, col_ids, picks_out, picks_in, c0, c1, d0, d1,
    stats_col, stats_row, m_col, m_full, sub_full, place, placed0, placed1,
    load_sem, send_col, recv_col, send_row, recv_row,
):
    me_p = lax.axis_index("row")
    me_q = lax.axis_index("col")
    per = LANES // slots

    load_rhs = pltpu.make_async_copy(rhs_hbm, rhs_v, load_sem.at[0])
    half = slots // 2
    load_tiles = [
        pltpu.make_async_copy(
            tiles_hbm.at[i * half : (i + 1) * half],
            tiles_v.at[:, :, i * LANES : (i + 1) * LANES],
            load_sem.at[1 + i],
        )
        for i in range(2)
    ]
    load_coords = pltpu.make_async_copy(coords_hbm, coords_v, load_sem.at[3])
    load_coords.start()
    load_rhs.start()
    for load in load_tiles:
        load.start()

    def row_peer(o):
        return (lax.rem(me_p + o, nr), me_q)

    def col_peer(o):
        return (me_p, lax.rem(me_q + o, nc))

    barrier = pltpu.get_barrier_semaphore()
    for o in range(1, nr):
        pl.semaphore_signal(
            barrier, inc=1, device_id=row_peer(o), device_id_type=pl.DeviceIdType.MESH
        )
    for o in range(1, nc):
        pl.semaphore_signal(
            barrier, inc=1, device_id=col_peer(o), device_id_type=pl.DeviceIdType.MESH
        )

    lane = iota((1, LANES), 1)
    load_coords.wait()
    numbers = jnp.concatenate([coords_v[...]] * per, axis=1)
    numbers = jnp.where(iota((2, LANES), 1) % slots < counts[0, 0], numbers, -1).astype(F32)
    row_ids[me_q] = numbers[0:1]
    col_ids[me_p] = numbers[1:2]

    pl.semaphore_wait(barrier, nr + nc - 2)

    sent = []

    def send_over_col(phase, source, mine):
        copies = []
        for o in range(1, nc):
            copy = pltpu.make_async_remote_copy(
                src_ref=source(lax.rem(me_q + o, nc)),
                dst_ref=mine,
                send_sem=send_col.at[phase, o - 1],
                recv_sem=recv_col.at[phase, o - 1],
                device_id=col_peer(o),
                device_id_type=pl.DeviceIdType.MESH,
            )
            copy.start()
            copies.append(copy)
        sent.extend(copies)
        return copies

    def send_over_row(phase, mine):
        copies = []
        for o in range(1, nr):
            copy = pltpu.make_async_remote_copy(
                src_ref=mine,
                dst_ref=mine,
                send_sem=send_row.at[phase, o - 1],
                recv_sem=recv_row.at[phase, o - 1],
                device_id=row_peer(o),
                device_id_type=pl.DeviceIdType.MESH,
            )
            copy.start()
            copies.append(copy)
        sent.extend(copies)
        return copies

    def arrived(copies):
        for copy in copies:
            copy.wait_recv()

    row_ids_copies = send_over_col(0, lambda peer: row_ids.at[me_q], row_ids.at[me_q])
    col_ids_copies = send_over_row(0, col_ids.at[me_p])

    load_rhs.wait()
    squares = []
    for r in range(2):
        part = rhs_v[pl.ds(r, range_len, stride=2), :].astype(BF)
        ub[:, r * LANES : (r + 1) * LANES] = part
        values = part.astype(F32)
        squares.append(total_of(values * values))

    arrived(row_ids_copies)

    def joined(ids_ref, g):
        ids = ids_ref[g * per]
        for j in range(1, per):
            ids = jnp.where(lane // slots == j, ids_ref[g * per + j], ids)
        return ids

    def upright(ids):
        return jnp.broadcast_to(ids, (LANES, LANES)).T

    row_lines = [joined(row_ids, g) for g in range(nc // per)]
    width = min(LANES, range_len)
    base = (me_q * range_len).astype(F32)
    for g in range(nc // per):
        local = upright(row_lines[g] - base)[:, :width]
        column = iota((LANES, width), 1).astype(F32)
        onehot = jnp.concatenate(
            [
                jnp.where(local == column + float(c * width), 1.0, 0.0).astype(BF)
                for c in range(range_len // width)
            ],
            axis=1,
        )
        taken = jnp.dot(onehot, ub[...], preferred_element_type=F32).astype(BF)
        for j in range(per):
            for r in range(2):
                picks_out[g * per + j, r * slots : (r + 1) * slots, :] = taken[
                    j * slots : (j + 1) * slots, r * LANES : (r + 1) * LANES
                ]
    picks_copies = send_over_col(1, lambda peer: picks_out.at[peer], picks_in.at[me_q])
    picks_in[me_q] = picks_out[me_q]

    for s in range(nc // per):
        sub = upright(row_lines[s])
        sub_full[s * LANES : (s + 1) * LANES, :] = sub
        for t in range(nc // per):
            line = row_lines[t]
            m_full[s * LANES : (s + 1) * LANES, t * LANES : (t + 1) * LANES] = jnp.where(
                (sub == line) & (line >= 0.0), 1.0, 0.0
            ).astype(BF)
    own_rows = pl.ds(pl.multiple_of(me_q * slots, slots), slots)
    m_row = m_full[own_rows, :]
    row_live = sub_full[own_rows, :] >= 0.0

    for load in load_tiles:
        load.wait()

    def turn(first, last):
        for k in range(first, last):
            for i in range(2):
                lanes = slice(i * LANES, (i + 1) * LANES)
                tt[k * LANES : (k + 1) * LANES, lanes] = (
                    tiles_v[k, :, lanes].astype(F32).T.astype(BF)
                )

    turn(0, half // 2)
    stacked = tiles_v[...].reshape(half * LANES, 2 * LANES)

    def over_row(phase, buffer, r, values, blocks):
        own = diagonal_dot(values, blocks, slots).astype(BF)
        buffer[r, me_p] = own
        return own, send_over_row(phase + r, buffer.at[r, me_p])

    def over_col(phase, buffer, r, values, blocks):
        own = diagonal_dot(values, blocks, slots).astype(BF)
        buffer[r, me_q] = own
        return own, send_over_col(
            phase + r, lambda peer: buffer.at[r, me_q], buffer.at[r, me_q]
        )

    def total(matches, buffer, r):
        return jnp.dot(
            matches, buffer[r].reshape(-1, LANES), preferred_element_type=F32
        )

    def inner(own, summed, live):
        return total_of(jnp.where(live, own.astype(F32) * summed, 0.0))

    arrived(picks_copies)
    c0_sent = []
    for r in range(2):
        u0 = picks_in[0, r * slots : (r + 1) * slots, :].astype(F32)
        for j in range(1, nc):
            u0 = u0 + picks_in[j, r * slots : (r + 1) * slots, :].astype(F32)
        c0_sent.append(over_row(1, c0, r, u0, stacked))

    turn(half // 2, half)
    arrived(col_ids_copies)
    sub_col = upright(col_ids[me_p])[:slots]
    col_live = sub_col >= 0.0
    col_lines = [joined(col_ids, g) for g in range(nr // per)]
    for s in range(nr // per):
        line = col_lines[s]
        m_col[:, s * LANES : (s + 1) * LANES] = jnp.where(
            (sub_col == line) & (line >= 0.0), 1.0, 0.0
        ).astype(BF)
    col_base = (me_p * range_len).astype(F32)
    chunk = min(256, range_len)
    for start in range(0, range_len, chunk):
        number = (iota((chunk, LANES), 0) + start).astype(F32)
        for s in range(nr // per):
            place[start : start + chunk, s * LANES : (s + 1) * LANES] = jnp.where(
                number == col_lines[s] - col_base, 1.0, 0.0
            ).astype(BF)

    def put(buffer, target):
        both = jnp.concatenate([buffer[r].reshape(nr * slots, LANES) for r in range(2)], axis=1)
        for start in range(0, range_len, chunk):
            target[start : start + chunk, :] = jnp.dot(
                place[start : start + chunk, :], both, preferred_element_type=F32
            )

    g0, d0_sent = [], []
    for r in range(2):
        arrived(c0_sent[r][1])
        g0.append(total(m_col[...], c0, r))
        d0_sent.append(over_col(2, d0, r, g0[r], tt[...]))
    gg = [inner(c0_sent[r][0], g0[r], col_live) for r in range(2)]

    f0, c1_sent = [], []
    for r in range(2):
        arrived(d0_sent[r][1])
        f0.append(total(m_row, d0, r))
        c1_sent.append(over_row(3, c1, r, f0[r], stacked))
    ff = [inner(d0_sent[r][0], f0[r], row_live) for r in range(2)]
    put(c0, placed0)

    g1, d1_sent = [], []
    for r in range(2):
        arrived(c1_sent[r][1])
        g1.append(total(m_col[...], c1, r))
        d1_sent.append(over_col(4, d1, r, g1[r], tt[...]))
    hh = [inner(c1_sent[r][0], g1[r], col_live) for r in range(2)]

    stats = jnp.zeros((1, LANES), F32)
    for s, pair in enumerate((squares, gg, ff, hh)):
        for r in range(2):
            stats = jnp.where(lane == 2 * s + r, pair[r], stats)
    stats_col[me_q] = stats
    stats_col_copies = send_over_col(6, lambda peer: stats_col.at[me_q], stats_col.at[me_q])

    full_live = sub_full[...] >= 0.0
    ee = []
    for r in range(2):
        arrived(d1_sent[r][1])
        f1 = total(m_full[...], d1, r)
        ee.append(inner(d1[r].reshape(nc * slots, LANES), f1, full_live))
    arrived(stats_col_copies)
    group = jnp.sum(stats_col[...], axis=0)
    for r in range(2):
        group = jnp.where(lane == 8 + r, ee[r], group)
    stats_row[me_p] = group
    stats_row_copies = send_over_row(5, stats_row.at[me_p])
    put(c1, placed1)
    arrived(stats_row_copies)
    whole = jnp.sum(stats_row[...], axis=0)

    uu, gg, ff, hh, ee = [whole] + [pltpu.roll(whole, LANES - 2 * s, 1) for s in range(1, 5)]

    def norm(square):
        return jnp.sqrt(jnp.maximum(square, 0.0) + EPS)

    beta0 = norm(uu)
    alpha0 = norm(gg / (beta0 * beta0))
    a = 1.0 / (beta0 * alpha0)
    b = alpha0 / beta0
    beta1 = norm(a * a * ff - 2.0 * (a * b) * gg + b * b * uu)
    rho0 = jnp.sqrt(alpha0 * alpha0 + beta1 * beta1)
    cosine = alpha0 / rho0
    sine = beta1 / rho0
    phi0 = cosine * beta0
    phi_bar = sine * beta0
    x = a / beta1
    y = -(b / beta1 + beta1 * a)
    alpha1 = norm(x * x * hh + 2.0 * (x * y) * ff + y * y * gg)
    theta = sine * alpha1
    rho_bar = -cosine * alpha1
    e = x / alpha1
    h = y / alpha1 - (alpha1 / beta1) * a
    w = (alpha1 / beta1) * b
    beta2 = norm(
        e * e * ee + h * h * ff + w * w * uu
        + 2.0 * (e * h) * hh + 2.0 * (e * w) * ff + 2.0 * (h * w) * gg
    )
    rho1 = jnp.sqrt(rho_bar * rho_bar + beta2 * beta2)
    phi1 = (rho_bar / rho1) * phi_bar
    phi_ref[...] = ((beta2 / rho1) * phi_bar)[:, 0:2]
    on_g1 = (phi1 / rho1) * e
    on_g0 = (phi0 / rho0) * a + (phi1 / rho1) * (y / alpha1 - (theta / rho0) * a)

    for start in range(0, range_len, chunk):
        here = slice(start, start + chunk)
        for r in range(2):
            lanes = slice(r * LANES, (r + 1) * LANES)
            out_ref[pl.ds(2 * start + r, chunk, stride=2), :] = (
                placed0[here, lanes] * on_g0[:, r : r + 1]
                + placed1[here, lanes] * on_g1[:, r : r + 1]
            )

    for copy in sent:
        copy.wait_send()


def on_device(nr, nc, tiles, coords, counts, rhs):
    slots, block = tiles.shape[2], tiles.shape[3]
    range_len = rhs.shape[1] // block
    piece = rhs.reshape(2, range_len, block).transpose(1, 0, 2).reshape(2 * range_len, block)
    dma = pltpu.SemaphoreType.DMA
    placed, phi = pl.pallas_call(
        functools.partial(solver, nr, nc, slots, range_len),
        out_shape=(
            jax.ShapeDtypeStruct((2 * range_len, block), F32),
            jax.ShapeDtypeStruct((1, 2), F32),
        ),
        in_specs=[
            pl.BlockSpec(memory_space=pltpu.HBM),
            pl.BlockSpec(memory_space=pltpu.SMEM),
            pl.BlockSpec(memory_space=pltpu.HBM),
            pl.BlockSpec(memory_space=pltpu.HBM),
        ],
        out_specs=(
            pl.BlockSpec(memory_space=pltpu.VMEM),
            pl.BlockSpec(memory_space=pltpu.VMEM),
        ),
        scratch_shapes=[
            pltpu.VMEM((2, slots), jnp.int32),
            pltpu.VMEM((2 * range_len, block), F32),
            pltpu.VMEM((range_len, 2 * block), BF),
            pltpu.VMEM((slots // 2, block, 2 * block), BF),
            pltpu.VMEM((slots // 2 * block, 2 * block), BF),
            pltpu.VMEM((nc, 1, LANES), F32),
            pltpu.VMEM((nr, 1, LANES), F32),
            pltpu.VMEM((nc, 2 * slots, block), BF),
            pltpu.VMEM((nc, 2 * slots, block), BF),
            pltpu.VMEM((2, nr, slots, block), BF),
            pltpu.VMEM((2, nr, slots, block), BF),
            pltpu.VMEM((2, nc, slots, block), BF),
            pltpu.VMEM((2, nc, slots, block), BF),
            pltpu.VMEM((nc, 1, LANES), F32),
            pltpu.VMEM((nr, 1, LANES), F32),
            pltpu.VMEM((slots, nr * slots), BF),
            pltpu.VMEM((nc * slots, nc * slots), BF),
            pltpu.VMEM((nc * slots, LANES), F32),
            pltpu.VMEM((range_len, nr * slots), BF),
            pltpu.VMEM((range_len, 2 * block), F32),
            pltpu.VMEM((range_len, 2 * block), F32),
            dma((4,)),
            dma((7, nc - 1)),
            dma((7, nc - 1)),
            dma((6, nr - 1)),
            dma((6, nr - 1)),
        ],
        compiler_params=pltpu.CompilerParams(
            collective_id=0, has_side_effects=True, vmem_limit_bytes=48 * 1024 * 1024
        ),
    )(
        pltpu.with_memory_space_constraint(coords[0, 0].T, pltpu.HBM),
        counts,
        pltpu.with_memory_space_constraint(tiles[0, 0], pltpu.HBM),
        pltpu.with_memory_space_constraint(piece, pltpu.HBM),
    )
    answer = placed.reshape(range_len, 2, block).transpose(1, 0, 2).reshape(2, range_len * block)
    return answer, phi[0]


def solution(mesh):
    nr, nc = mesh.shape["row"], mesh.shape["col"]
    return jax.shard_map(
        functools.partial(on_device, nr, nc),
        mesh=mesh,
        in_specs=(
            P("row", "col", None, None, None),
            P("row", "col", None, None),
            P("row", "col"),
            P(None, ("row", "col")),
        ),
        out_specs=(P(None, ("col", "row")), P()),
        check_vma=False,
    )
```

```python
import functools

import jax
import jax.numpy as jnp
from jax import lax
from jax.experimental import pallas as pl
from jax.experimental.pallas import tpu as pltpu
from jax.sharding import PartitionSpec as P

EPS = 1e-06
LANES = 128
BF = jnp.bfloat16
F32 = jnp.float32


def iota(shape, dim):
    return lax.broadcasted_iota(jnp.int32, shape, dim)


def diagonal_dot(values, stacked, slots):
    group, half = 8, slots // 2
    row_slot = iota((2 * group, LANES), 0) % group
    first, second = [], []
    for start in range(0, half, group):
        pair = jnp.concatenate(
            [values[start : start + group], values[half + start : half + start + group]], axis=0
        )
        wide = jnp.concatenate(
            [jnp.where(row_slot == k, pair, 0.0).astype(BF) for k in range(group)], axis=1
        )
        result = jnp.dot(
            wide,
            stacked[start * LANES : (start + group) * LANES],
            preferred_element_type=F32,
        )
        first.append(result[:group, :LANES])
        second.append(result[group:, LANES:])
    return jnp.concatenate(first + second, axis=0)


def total_of(products):
    line = jnp.sum(products, axis=0, keepdims=True)
    return jnp.sum(line, axis=1, keepdims=True)


def solver(
    nr, nc, slots, range_len,
    coords_hbm, counts, tiles_hbm, rhs_hbm,
    out_ref, phi_ref,
    coords_v, rhs_v, ub, tiles_v, tt, row_ids, col_ids, picks_out, picks_in, c0, c1, d0, d1,
    stats_col, stats_row, m_col, m_full, sub_full, place, placed0, placed1,
    load_sem, send_col, recv_col, send_row, recv_row,
):
    me_p = lax.axis_index("row")
    me_q = lax.axis_index("col")
    per = LANES // slots

    load_rhs = pltpu.make_async_copy(rhs_hbm, rhs_v, load_sem.at[0])
    half = slots // 2
    load_tiles = [
        pltpu.make_async_copy(
            tiles_hbm.at[i * half : (i + 1) * half],
            tiles_v.at[:, :, i * LANES : (i + 1) * LANES],
            load_sem.at[1 + i],
        )
        for i in range(2)
    ]
    load_coords = pltpu.make_async_copy(coords_hbm, coords_v, load_sem.at[3])
    load_coords.start()
    load_rhs.start()
    for load in load_tiles:
        load.start()

    def row_peer(o):
        return (lax.rem(me_p + o, nr), me_q)

    def col_peer(o):
        return (me_p, lax.rem(me_q + o, nc))

    barrier = pltpu.get_barrier_semaphore()
    for o in range(1, nr):
        pl.semaphore_signal(
            barrier, inc=1, device_id=row_peer(o), device_id_type=pl.DeviceIdType.MESH
        )
    for o in range(1, nc):
        pl.semaphore_signal(
            barrier, inc=1, device_id=col_peer(o), device_id_type=pl.DeviceIdType.MESH
        )

    lane = iota((1, LANES), 1)
    load_coords.wait()
    numbers = jnp.concatenate([coords_v[...]] * per, axis=1)
    numbers = jnp.where(iota((2, LANES), 1) % slots < counts[0, 0], numbers, -1).astype(F32)
    row_ids[me_q] = numbers[0:1]
    col_ids[me_p] = numbers[1:2]

    pl.semaphore_wait(barrier, nr + nc - 2)

    sent = []

    def send_over_col(phase, source, mine):
        copies = []
        for o in sorted(range(1, nc), key=lambda o: abs(2 * o - nc)):
            copy = pltpu.make_async_remote_copy(
                src_ref=source(lax.rem(me_q + o, nc)),
                dst_ref=mine,
                send_sem=send_col.at[phase, o - 1],
                recv_sem=recv_col.at[phase, o - 1],
                device_id=col_peer(o),
                device_id_type=pl.DeviceIdType.MESH,
            )
            copy.start()
            copies.append(copy)
        sent.extend(copies)
        return copies

    def send_over_row(phase, mine):
        copies = []
        for o in sorted(range(1, nr), key=lambda o: abs(2 * o - nr)):
            copy = pltpu.make_async_remote_copy(
                src_ref=mine,
                dst_ref=mine,
                send_sem=send_row.at[phase, o - 1],
                recv_sem=recv_row.at[phase, o - 1],
                device_id=row_peer(o),
                device_id_type=pl.DeviceIdType.MESH,
            )
            copy.start()
            copies.append(copy)
        sent.extend(copies)
        return copies

    def arrived(copies):
        for copy in copies:
            copy.wait_recv()

    row_ids_copies = send_over_col(0, lambda peer: row_ids.at[me_q], row_ids.at[me_q])
    col_ids_copies = send_over_row(0, col_ids.at[me_p])

    load_rhs.wait()
    squares = []
    for r in range(2):
        part = rhs_v[pl.ds(r, range_len, stride=2), :].astype(BF)
        ub[:, r * LANES : (r + 1) * LANES] = part
        values = part.astype(F32)
        squares.append(total_of(values * values))

    arrived(row_ids_copies)

    def joined(ids_ref, g):
        ids = ids_ref[g * per]
        for j in range(1, per):
            ids = jnp.where(lane // slots == j, ids_ref[g * per + j], ids)
        return ids

    def upright(ids):
        return jnp.broadcast_to(ids, (LANES, LANES)).T

    row_lines = [joined(row_ids, g) for g in range(nc // per)]
    width = min(LANES, range_len)
    base = (me_q * range_len).astype(F32)
    for g in range(nc // per):
        local = upright(row_lines[g] - base)[:, :width]
        column = iota((LANES, width), 1).astype(F32)
        onehot = jnp.concatenate(
            [
                jnp.where(local == column + float(c * width), 1.0, 0.0).astype(BF)
                for c in range(range_len // width)
            ],
            axis=1,
        )
        taken = jnp.dot(onehot, ub[...], preferred_element_type=F32).astype(BF)
        for j in range(per):
            for r in range(2):
                picks_out[g * per + j, r * slots : (r + 1) * slots, :] = taken[
                    j * slots : (j + 1) * slots, r * LANES : (r + 1) * LANES
                ]
    picks_copies = send_over_col(1, lambda peer: picks_out.at[peer], picks_in.at[me_q])
    picks_in[me_q] = picks_out[me_q]

    for s in range(nc // per):
        sub = upright(row_lines[s])
        sub_full[s * LANES : (s + 1) * LANES, :] = sub
        for t in range(nc // per):
            line = row_lines[t]
            m_full[s * LANES : (s + 1) * LANES, t * LANES : (t + 1) * LANES] = jnp.where(
                (sub == line) & (line >= 0.0), 1.0, 0.0
            ).astype(BF)
    own_rows = pl.ds(pl.multiple_of(me_q * slots, slots), slots)
    m_row = m_full[own_rows, :]
    row_live = sub_full[own_rows, :] >= 0.0

    for load in load_tiles:
        load.wait()

    def turn(first, last):
        for k in range(first, last):
            for i in range(2):
                lanes = slice(i * LANES, (i + 1) * LANES)
                tt[k * LANES : (k + 1) * LANES, lanes] = (
                    tiles_v[k, :, lanes].T
                )

    turn(0, half // 4)
    stacked = tiles_v[...].reshape(half * LANES, 2 * LANES)

    def over_row(phase, buffer, r, values, blocks):
        own = diagonal_dot(values, blocks, slots).astype(BF)
        buffer[r, me_p] = own
        return own, send_over_row(phase + r, buffer.at[r, me_p])

    def over_col(phase, buffer, r, values, blocks):
        own = diagonal_dot(values, blocks, slots).astype(BF)
        buffer[r, me_q] = own
        return own, send_over_col(
            phase + r, lambda peer: buffer.at[r, me_q], buffer.at[r, me_q]
        )

    def total(matches, buffer, r):
        return jnp.dot(
            matches, buffer[r].reshape(-1, LANES), preferred_element_type=F32
        )

    def inner(own, summed, live):
        return total_of(jnp.where(live, own.astype(F32) * summed, 0.0))

    arrived(picks_copies)
    c0_sent = []
    for r in range(2):
        u0 = picks_in[0, r * slots : (r + 1) * slots, :].astype(F32)
        for j in range(1, nc):
            u0 = u0 + picks_in[j, r * slots : (r + 1) * slots, :].astype(F32)
        c0_sent.append(over_row(1, c0, r, u0, stacked))

    turn(half // 4, half)
    arrived(col_ids_copies)
    sub_col = upright(col_ids[me_p])[:slots]
    col_live = sub_col >= 0.0
    col_lines = [joined(col_ids, g) for g in range(nr // per)]
    for s in range(nr // per):
        line = col_lines[s]
        m_col[:, s * LANES : (s + 1) * LANES] = jnp.where(
            (sub_col == line) & (line >= 0.0), 1.0, 0.0
        ).astype(BF)
    chunk = min(256, range_len)

    def put(buffer, target):
        both = jnp.concatenate([buffer[r].reshape(nr * slots, LANES) for r in range(2)], axis=1)
        for start in range(0, range_len, chunk):
            target[start : start + chunk, :] = jnp.dot(
                place[start : start + chunk, :], both, preferred_element_type=F32
            )

    g0, d0_sent = [], []
    for r in range(2):
        arrived(c0_sent[r][1])
        g0.append(total(m_col[...], c0, r))
        d0_sent.append(over_col(2, d0, r, g0[r], tt[...]))
    gg = [inner(c0_sent[r][0], g0[r], col_live) for r in range(2)]

    f0, c1_sent = [], []
    for r in range(2):
        arrived(d0_sent[r][1])
        f0.append(total(m_row, d0, r))
        c1_sent.append(over_row(3, c1, r, f0[r], stacked))
    ff = [inner(d0_sent[r][0], f0[r], row_live) for r in range(2)]
    col_base = (me_p * range_len).astype(F32)
    for start in range(0, range_len, chunk):
        number = (iota((chunk, LANES), 0) + start).astype(F32)
        for s in range(nr // per):
            place[start : start + chunk, s * LANES : (s + 1) * LANES] = jnp.where(
                number == col_lines[s] - col_base, 1.0, 0.0
            ).astype(BF)
    put(c0, placed0)

    g1, d1_sent = [], []
    for r in range(2):
        arrived(c1_sent[r][1])
        g1.append(total(m_col[...], c1, r))
        d1_sent.append(over_col(4, d1, r, g1[r], tt[...]))
    hh = [inner(c1_sent[r][0], g1[r], col_live) for r in range(2)]

    stats = jnp.zeros((1, LANES), F32)
    for s, pair in enumerate((squares, gg, ff, hh)):
        for r in range(2):
            stats = jnp.where(lane == 2 * s + r, pair[r], stats)
    stats_col[me_q] = stats
    stats_col_copies = send_over_col(6, lambda peer: stats_col.at[me_q], stats_col.at[me_q])

    full_live = sub_full[...] >= 0.0
    ee = []
    for r in range(2):
        arrived(d1_sent[r][1])
        f1 = total(m_full[...], d1, r)
        ee.append(inner(d1[r].reshape(nc * slots, LANES), f1, full_live))
    arrived(stats_col_copies)
    group = jnp.sum(stats_col[...], axis=0)
    for r in range(2):
        group = jnp.where(lane == 8 + r, ee[r], group)
    stats_row[me_p] = group
    earlier = list(sent)
    stats_row_copies = send_over_row(5, stats_row.at[me_p])
    put(c1, placed1)
    for copy in earlier:
        copy.wait_send()
    arrived(stats_row_copies)
    whole = jnp.sum(stats_row[...], axis=0)

    uu, gg, ff, hh, ee = [whole] + [pltpu.roll(whole, LANES - 2 * s, 1) for s in range(1, 5)]

    def norm(square):
        return jnp.sqrt(jnp.maximum(square, 0.0) + EPS)

    beta0 = norm(uu)
    alpha0 = norm(gg / (beta0 * beta0))
    a = 1.0 / (beta0 * alpha0)
    b = alpha0 / beta0
    beta1 = norm(a * a * ff - 2.0 * (a * b) * gg + b * b * uu)
    rho0 = jnp.sqrt(alpha0 * alpha0 + beta1 * beta1)
    cosine = alpha0 / rho0
    sine = beta1 / rho0
    phi0 = cosine * beta0
    phi_bar = sine * beta0
    x = a / beta1
    y = -(b / beta1 + beta1 * a)
    alpha1 = norm(x * x * hh + 2.0 * (x * y) * ff + y * y * gg)
    theta = sine * alpha1
    rho_bar = -cosine * alpha1
    e = x / alpha1
    h = y / alpha1 - (alpha1 / beta1) * a
    w = (alpha1 / beta1) * b
    beta2 = norm(
        e * e * ee + h * h * ff + w * w * uu
        + 2.0 * (e * h) * hh + 2.0 * (e * w) * ff + 2.0 * (h * w) * gg
    )
    rho1 = jnp.sqrt(rho_bar * rho_bar + beta2 * beta2)
    phi1 = (rho_bar / rho1) * phi_bar
    phi_ref[...] = ((beta2 / rho1) * phi_bar)[:, 0:2]
    on_g1 = (phi1 / rho1) * e
    on_g0 = (phi0 / rho0) * a + (phi1 / rho1) * (y / alpha1 - (theta / rho0) * a)

    for start in range(0, range_len, chunk):
        here = slice(start, start + chunk)
        for r in range(2):
            lanes = slice(r * LANES, (r + 1) * LANES)
            out_ref[pl.ds(2 * start + r, chunk, stride=2), :] = (
                placed0[here, lanes] * on_g0[:, r : r + 1]
                + placed1[here, lanes] * on_g1[:, r : r + 1]
            )

    for copy in stats_row_copies:
        copy.wait_send()


def on_device(nr, nc, tiles, coords, counts, rhs):
    slots, block = tiles.shape[2], tiles.shape[3]
    range_len = rhs.shape[1] // block
    piece = rhs.reshape(2, range_len, block).transpose(1, 0, 2).reshape(2 * range_len, block)
    dma = pltpu.SemaphoreType.DMA
    placed, phi = pl.pallas_call(
        functools.partial(solver, nr, nc, slots, range_len),
        out_shape=(
            jax.ShapeDtypeStruct((2 * range_len, block), F32),
            jax.ShapeDtypeStruct((1, 2), F32),
        ),
        in_specs=[
            pl.BlockSpec(memory_space=pltpu.HBM),
            pl.BlockSpec(memory_space=pltpu.SMEM),
            pl.BlockSpec(memory_space=pltpu.HBM),
            pl.BlockSpec(memory_space=pltpu.HBM),
        ],
        out_specs=(
            pl.BlockSpec(memory_space=pltpu.VMEM),
            pl.BlockSpec(memory_space=pltpu.VMEM),
        ),
        scratch_shapes=[
            pltpu.VMEM((2, slots), jnp.int32),
            pltpu.VMEM((2 * range_len, block), F32),
            pltpu.VMEM((range_len, 2 * block), BF),
            pltpu.VMEM((slots // 2, block, 2 * block), BF),
            pltpu.VMEM((slots // 2 * block, 2 * block), BF),
            pltpu.VMEM((nc, 1, LANES), F32),
            pltpu.VMEM((nr, 1, LANES), F32),
            pltpu.VMEM((nc, 2 * slots, block), BF),
            pltpu.VMEM((nc, 2 * slots, block), BF),
            pltpu.VMEM((2, nr, slots, block), BF),
            pltpu.VMEM((2, nr, slots, block), BF),
            pltpu.VMEM((2, nc, slots, block), BF),
            pltpu.VMEM((2, nc, slots, block), BF),
            pltpu.VMEM((nc, 1, LANES), F32),
            pltpu.VMEM((nr, 1, LANES), F32),
            pltpu.VMEM((slots, nr * slots), BF),
            pltpu.VMEM((nc * slots, nc * slots), BF),
            pltpu.VMEM((nc * slots, LANES), F32),
            pltpu.VMEM((range_len, nr * slots), BF),
            pltpu.VMEM((range_len, 2 * block), F32),
            pltpu.VMEM((range_len, 2 * block), F32),
            dma((4,)),
            dma((7, nc - 1)),
            dma((7, nc - 1)),
            dma((6, nr - 1)),
            dma((6, nr - 1)),
        ],
        compiler_params=pltpu.CompilerParams(
            collective_id=0, has_side_effects=True, vmem_limit_bytes=48 * 1024 * 1024
        ),
    )(
        pltpu.with_memory_space_constraint(coords[0, 0].T, pltpu.HBM),
        counts,
        pltpu.with_memory_space_constraint(tiles[0, 0], pltpu.HBM),
        pltpu.with_memory_space_constraint(piece, pltpu.HBM),
    )
    answer = placed.reshape(range_len, 2, block).transpose(1, 0, 2).reshape(2, range_len * block)
    return answer, phi[0]


def solution(mesh):
    nr, nc = mesh.shape["row"], mesh.shape["col"]
    return jax.shard_map(
        functools.partial(on_device, nr, nc),
        mesh=mesh,
        in_specs=(
            P("row", "col", None, None, None),
            P("row", "col", None, None),
            P("row", "col"),
            P(None, ("row", "col")),
        ),
        out_specs=(P(None, ("col", "row")), P()),
        check_vma=False,
    )
```

```python
import functools

import jax
import jax.numpy as jnp
from jax import lax
from jax.experimental import pallas as pl
from jax.experimental.pallas import tpu as pltpu
from jax.sharding import PartitionSpec as P

EPS = 1e-06
LANES = 128
BF = jnp.bfloat16
F32 = jnp.float32


def iota(shape, dim):
    return lax.broadcasted_iota(jnp.int32, shape, dim)


def diagonal_dot(values, stacked, slots):
    group, half = 8, slots // 2
    row_slot = iota((4 * group, LANES), 0) % group
    parts = []
    for start in range(0, half, group):
        quad = jnp.concatenate(
            [v[i + start : i + start + group] for v in values for i in (0, half)], axis=0
        )
        wide = jnp.concatenate(
            [jnp.where(row_slot == k, quad, 0.0).astype(BF) for k in range(group)], axis=1
        )
        parts.append(
            jnp.dot(
                wide,
                stacked[start * LANES : (start + group) * LANES],
                preferred_element_type=F32,
            )
        )
    pieces = []
    for r in range(2):
        for i in range(2):
            at = (2 * r + i) * group
            pieces += [p[at : at + group, i * LANES : (i + 1) * LANES] for p in parts]
    return jnp.concatenate(pieces, axis=0)


def total_of(products):
    line = jnp.sum(products, axis=0, keepdims=True)
    return jnp.sum(line, axis=1, keepdims=True)


def solver(
    nr, nc, slots, range_len,
    coords_hbm, counts, tiles_hbm, rhs_hbm,
    out_ref, phi_ref,
    coords_v, rhs_v, ub, tiles_v, tt, row_ids, col_ids, picks_out, picks_in, c0, c1, d0, d1,
    stats_col, stats_row, m_col, m_full, sub_full, place, placed0, placed1,
    load_sem, send_col, recv_col, send_row, recv_row,
):
    me_p = lax.axis_index("row")
    me_q = lax.axis_index("col")
    per = LANES // slots

    load_rhs = pltpu.make_async_copy(rhs_hbm, rhs_v, load_sem.at[0])
    half = slots // 2
    load_tiles = [
        pltpu.make_async_copy(
            tiles_hbm.at[i * half : (i + 1) * half],
            tiles_v.at[:, :, i * LANES : (i + 1) * LANES],
            load_sem.at[1 + i],
        )
        for i in range(2)
    ]
    load_coords = pltpu.make_async_copy(coords_hbm, coords_v, load_sem.at[3])
    load_coords.start()
    load_rhs.start()
    for load in load_tiles:
        load.start()

    def row_peer(o):
        return (lax.rem(me_p + o, nr), me_q)

    def col_peer(o):
        return (me_p, lax.rem(me_q + o, nc))

    barrier = pltpu.get_barrier_semaphore()
    for o in range(1, nr):
        pl.semaphore_signal(
            barrier, inc=1, device_id=row_peer(o), device_id_type=pl.DeviceIdType.MESH
        )
    for o in range(1, nc):
        pl.semaphore_signal(
            barrier, inc=1, device_id=col_peer(o), device_id_type=pl.DeviceIdType.MESH
        )

    lane = iota((1, LANES), 1)
    load_coords.wait()
    numbers = jnp.concatenate([coords_v[...]] * per, axis=1)
    numbers = jnp.where(iota((2, LANES), 1) % slots < counts[0, 0], numbers, -1).astype(F32)
    row_ids[me_q] = numbers[0:1]
    col_ids[me_p] = numbers[1:2]

    pl.semaphore_wait(barrier, nr + nc - 2)

    sent = []

    def send_over_col(phase, source, mine):
        copies = []
        for o in sorted(range(1, nc), key=lambda o: abs(2 * o - nc)):
            copy = pltpu.make_async_remote_copy(
                src_ref=source(lax.rem(me_q + o, nc)),
                dst_ref=mine,
                send_sem=send_col.at[phase, o - 1],
                recv_sem=recv_col.at[phase, o - 1],
                device_id=col_peer(o),
                device_id_type=pl.DeviceIdType.MESH,
            )
            copy.start()
            copies.append(copy)
        sent.extend(copies)
        return copies

    def send_over_row(phase, mine):
        copies = []
        for o in sorted(range(1, nr), key=lambda o: abs(2 * o - nr)):
            copy = pltpu.make_async_remote_copy(
                src_ref=mine,
                dst_ref=mine,
                send_sem=send_row.at[phase, o - 1],
                recv_sem=recv_row.at[phase, o - 1],
                device_id=row_peer(o),
                device_id_type=pl.DeviceIdType.MESH,
            )
            copy.start()
            copies.append(copy)
        sent.extend(copies)
        return copies

    def arrived(copies):
        for copy in copies:
            copy.wait_recv()

    row_ids_copies = send_over_col(0, lambda peer: row_ids.at[me_q], row_ids.at[me_q])
    col_ids_copies = send_over_row(0, col_ids.at[me_p])

    load_rhs.wait()
    squares = []
    for r in range(2):
        part = rhs_v[pl.ds(r, range_len, stride=2), :].astype(BF)
        ub[:, r * LANES : (r + 1) * LANES] = part
        values = part.astype(F32)
        squares.append(total_of(values * values))

    arrived(row_ids_copies)

    def joined(ids_ref, g):
        ids = ids_ref[g * per]
        for j in range(1, per):
            ids = jnp.where(lane // slots == j, ids_ref[g * per + j], ids)
        return ids

    def upright(ids):
        return jnp.broadcast_to(ids, (LANES, LANES)).T

    row_lines = [joined(row_ids, g) for g in range(nc // per)]
    width = min(LANES, range_len)
    base = (me_q * range_len).astype(F32)
    for g in range(nc // per):
        local = upright(row_lines[g] - base)[:, :width]
        column = iota((LANES, width), 1).astype(F32)
        onehot = jnp.concatenate(
            [
                jnp.where(local == column + float(c * width), 1.0, 0.0).astype(BF)
                for c in range(range_len // width)
            ],
            axis=1,
        )
        taken = jnp.dot(onehot, ub[...], preferred_element_type=F32).astype(BF)
        for j in range(per):
            for r in range(2):
                picks_out[g * per + j, r * slots : (r + 1) * slots, :] = taken[
                    j * slots : (j + 1) * slots, r * LANES : (r + 1) * LANES
                ]
    picks_copies = send_over_col(1, lambda peer: picks_out.at[peer], picks_in.at[me_q])
    picks_in[me_q] = picks_out[me_q]

    for s in range(nc // per):
        sub = upright(row_lines[s])
        sub_full[s * LANES : (s + 1) * LANES, :] = sub
        for t in range(nc // per):
            line = row_lines[t]
            m_full[s * LANES : (s + 1) * LANES, t * LANES : (t + 1) * LANES] = jnp.where(
                (sub == line) & (line >= 0.0), 1.0, 0.0
            ).astype(BF)
    own_rows = pl.ds(pl.multiple_of(me_q * slots, slots), slots)
    m_row = m_full[own_rows, :]
    row_live = sub_full[own_rows, :] >= 0.0

    for load in load_tiles:
        load.wait()

    def turn(first, last):
        for k in range(first, last):
            for i in range(2):
                lanes = slice(i * LANES, (i + 1) * LANES)
                tt[k * LANES : (k + 1) * LANES, lanes] = (
                    tiles_v[k, :, lanes].T
                )

    turn(0, half // 4)
    stacked = tiles_v[...].reshape(half * LANES, 2 * LANES)

    def over_row(phase, buffer, values, blocks):
        own = diagonal_dot(values, blocks, slots).astype(BF)
        buffer[me_p] = own
        return own, send_over_row(phase, buffer.at[me_p])

    def over_col(phase, buffer, values, blocks):
        own = diagonal_dot(values, blocks, slots).astype(BF)
        buffer[me_q] = own
        return own, send_over_col(phase, lambda peer: buffer.at[me_q], buffer.at[me_q])

    def of(buffer, r):
        return buffer[:, r * slots : (r + 1) * slots, :].reshape(-1, LANES)

    def beside(buffer):
        return jnp.concatenate([of(buffer, r) for r in range(2)], axis=1)

    def total(matches, buffer):
        both = jnp.dot(matches, beside(buffer), preferred_element_type=F32)
        return [both[:, r * LANES : (r + 1) * LANES] for r in range(2)]

    def inner(own, summed, live):
        return total_of(jnp.where(live, own.astype(F32) * summed, 0.0))

    def inners(own, summed, live):
        return [inner(own[r * slots : (r + 1) * slots], summed[r], live) for r in range(2)]

    arrived(picks_copies)
    u0 = []
    for r in range(2):
        part = picks_in[0, r * slots : (r + 1) * slots, :].astype(F32)
        for j in range(1, nc):
            part = part + picks_in[j, r * slots : (r + 1) * slots, :].astype(F32)
        u0.append(part)
    c0_own, c0_copies = over_row(1, c0, u0, stacked)

    turn(half // 4, half)
    arrived(col_ids_copies)
    sub_col = upright(col_ids[me_p])[:slots]
    col_live = sub_col >= 0.0
    col_lines = [joined(col_ids, g) for g in range(nr // per)]
    for s in range(nr // per):
        line = col_lines[s]
        m_col[:, s * LANES : (s + 1) * LANES] = jnp.where(
            (sub_col == line) & (line >= 0.0), 1.0, 0.0
        ).astype(BF)
    chunk = min(256, range_len)

    def put(buffer, target):
        both = beside(buffer)
        for start in range(0, range_len, chunk):
            target[start : start + chunk, :] = jnp.dot(
                place[start : start + chunk, :], both, preferred_element_type=F32
            )

    arrived(c0_copies)
    g0 = total(m_col[...], c0)
    d0_own, d0_copies = over_col(2, d0, g0, tt[...])
    gg = inners(c0_own, g0, col_live)

    arrived(d0_copies)
    f0 = total(m_row, d0)
    c1_own, c1_copies = over_row(3, c1, f0, stacked)
    ff = inners(d0_own, f0, row_live)
    col_base = (me_p * range_len).astype(F32)
    for start in range(0, range_len, chunk):
        number = (iota((chunk, LANES), 0) + start).astype(F32)
        for s in range(nr // per):
            place[start : start + chunk, s * LANES : (s + 1) * LANES] = jnp.where(
                number == col_lines[s] - col_base, 1.0, 0.0
            ).astype(BF)
    put(c0, placed0)

    arrived(c1_copies)
    g1 = total(m_col[...], c1)
    d1_own, d1_copies = over_col(4, d1, g1, tt[...])
    hh = inners(c1_own, g1, col_live)

    stats = jnp.zeros((1, LANES), F32)
    for s, pair in enumerate((squares, gg, ff, hh)):
        for r in range(2):
            stats = jnp.where(lane == 2 * s + r, pair[r], stats)
    stats_col[me_q] = stats
    stats_col_copies = send_over_col(6, lambda peer: stats_col.at[me_q], stats_col.at[me_q])

    full_live = sub_full[...] >= 0.0
    arrived(d1_copies)
    f1 = total(m_full[...], d1)
    ee = [inner(of(d1, r), f1[r], full_live) for r in range(2)]
    arrived(stats_col_copies)
    group = jnp.sum(stats_col[...], axis=0)
    for r in range(2):
        group = jnp.where(lane == 8 + r, ee[r], group)
    stats_row[me_p] = group
    earlier = list(sent)
    stats_row_copies = send_over_row(5, stats_row.at[me_p])
    put(c1, placed1)
    for copy in earlier:
        copy.wait_send()
    arrived(stats_row_copies)
    whole = jnp.sum(stats_row[...], axis=0)

    uu, gg, ff, hh, ee = [whole] + [pltpu.roll(whole, LANES - 2 * s, 1) for s in range(1, 5)]

    def norm(square):
        return jnp.sqrt(jnp.maximum(square, 0.0) + EPS)

    beta0 = norm(uu)
    alpha0 = norm(gg / (beta0 * beta0))
    a = 1.0 / (beta0 * alpha0)
    b = alpha0 / beta0
    beta1 = norm(a * a * ff - 2.0 * (a * b) * gg + b * b * uu)
    rho0 = jnp.sqrt(alpha0 * alpha0 + beta1 * beta1)
    cosine = alpha0 / rho0
    sine = beta1 / rho0
    phi0 = cosine * beta0
    phi_bar = sine * beta0
    x = a / beta1
    y = -(b / beta1 + beta1 * a)
    alpha1 = norm(x * x * hh + 2.0 * (x * y) * ff + y * y * gg)
    theta = sine * alpha1
    rho_bar = -cosine * alpha1
    e = x / alpha1
    h = y / alpha1 - (alpha1 / beta1) * a
    w = (alpha1 / beta1) * b
    beta2 = norm(
        e * e * ee + h * h * ff + w * w * uu
        + 2.0 * (e * h) * hh + 2.0 * (e * w) * ff + 2.0 * (h * w) * gg
    )
    rho1 = jnp.sqrt(rho_bar * rho_bar + beta2 * beta2)
    phi1 = (rho_bar / rho1) * phi_bar
    phi_ref[...] = ((beta2 / rho1) * phi_bar)[:, 0:2]
    on_g1 = (phi1 / rho1) * e
    on_g0 = (phi0 / rho0) * a + (phi1 / rho1) * (y / alpha1 - (theta / rho0) * a)

    for start in range(0, range_len, chunk):
        here = slice(start, start + chunk)
        for r in range(2):
            lanes = slice(r * LANES, (r + 1) * LANES)
            out_ref[pl.ds(2 * start + r, chunk, stride=2), :] = (
                placed0[here, lanes] * on_g0[:, r : r + 1]
                + placed1[here, lanes] * on_g1[:, r : r + 1]
            )

    for copy in stats_row_copies:
        copy.wait_send()


def on_device(nr, nc, tiles, coords, counts, rhs):
    slots, block = tiles.shape[2], tiles.shape[3]
    range_len = rhs.shape[1] // block
    piece = rhs.reshape(2, range_len, block).transpose(1, 0, 2).reshape(2 * range_len, block)
    dma = pltpu.SemaphoreType.DMA
    placed, phi = pl.pallas_call(
        functools.partial(solver, nr, nc, slots, range_len),
        out_shape=(
            jax.ShapeDtypeStruct((2 * range_len, block), F32),
            jax.ShapeDtypeStruct((1, 2), F32),
        ),
        in_specs=[
            pl.BlockSpec(memory_space=pltpu.HBM),
            pl.BlockSpec(memory_space=pltpu.SMEM),
            pl.BlockSpec(memory_space=pltpu.HBM),
            pl.BlockSpec(memory_space=pltpu.HBM),
        ],
        out_specs=(
            pl.BlockSpec(memory_space=pltpu.VMEM),
            pl.BlockSpec(memory_space=pltpu.VMEM),
        ),
        scratch_shapes=[
            pltpu.VMEM((2, slots), jnp.int32),
            pltpu.VMEM((2 * range_len, block), F32),
            pltpu.VMEM((range_len, 2 * block), BF),
            pltpu.VMEM((slots // 2, block, 2 * block), BF),
            pltpu.VMEM((slots // 2 * block, 2 * block), BF),
            pltpu.VMEM((nc, 1, LANES), F32),
            pltpu.VMEM((nr, 1, LANES), F32),
            pltpu.VMEM((nc, 2 * slots, block), BF),
            pltpu.VMEM((nc, 2 * slots, block), BF),
            pltpu.VMEM((nr, 2 * slots, block), BF),
            pltpu.VMEM((nr, 2 * slots, block), BF),
            pltpu.VMEM((nc, 2 * slots, block), BF),
            pltpu.VMEM((nc, 2 * slots, block), BF),
            pltpu.VMEM((nc, 1, LANES), F32),
            pltpu.VMEM((nr, 1, LANES), F32),
            pltpu.VMEM((slots, nr * slots), BF),
            pltpu.VMEM((nc * slots, nc * slots), BF),
            pltpu.VMEM((nc * slots, LANES), F32),
            pltpu.VMEM((range_len, nr * slots), BF),
            pltpu.VMEM((range_len, 2 * block), F32),
            pltpu.VMEM((range_len, 2 * block), F32),
            dma((4,)),
            dma((7, nc - 1)),
            dma((7, nc - 1)),
            dma((6, nr - 1)),
            dma((6, nr - 1)),
        ],
        compiler_params=pltpu.CompilerParams(
            collective_id=0, has_side_effects=True, vmem_limit_bytes=48 * 1024 * 1024
        ),
    )(
        pltpu.with_memory_space_constraint(coords[0, 0].T, pltpu.HBM),
        counts,
        pltpu.with_memory_space_constraint(tiles[0, 0], pltpu.HBM),
        pltpu.with_memory_space_constraint(piece, pltpu.HBM),
    )
    answer = placed.reshape(range_len, 2, block).transpose(1, 0, 2).reshape(2, range_len * block)
    return answer, phi[0]


def solution(mesh):
    nr, nc = mesh.shape["row"], mesh.shape["col"]
    return jax.shard_map(
        functools.partial(on_device, nr, nc),
        mesh=mesh,
        in_specs=(
            P("row", "col", None, None, None),
            P("row", "col", None, None),
            P("row", "col"),
            P(None, ("row", "col")),
        ),
        out_specs=(P(None, ("col", "row")), P()),
        check_vma=False,
    )
```

```python
import functools

import jax
import jax.numpy as jnp
from jax import lax
from jax.experimental import pallas as pl
from jax.experimental.pallas import tpu as pltpu
from jax.sharding import PartitionSpec as P

EPS = 1e-06
LANES = 128
BF = jnp.bfloat16
F32 = jnp.float32


def iota(shape, dim):
    return lax.broadcasted_iota(jnp.int32, shape, dim)


def diagonal_dot(values, stacked, slots):
    group, half = 8, slots // 2
    row_slot = iota((2 * group, LANES), 0) % group
    first, second = [], []
    for start in range(0, half, group):
        pair = jnp.concatenate(
            [values[start : start + group], values[half + start : half + start + group]], axis=0
        )
        wide = jnp.concatenate(
            [jnp.where(row_slot == k, pair, 0.0).astype(BF) for k in range(group)], axis=1
        )
        result = jnp.dot(
            wide,
            stacked[start * LANES : (start + group) * LANES],
            preferred_element_type=F32,
        )
        first.append(result[:group, :LANES])
        second.append(result[group:, LANES:])
    return jnp.concatenate(first + second, axis=0)


def total_of(products):
    line = jnp.sum(products, axis=0, keepdims=True)
    return jnp.sum(line, axis=1, keepdims=True)


def solver(
    nr, nc, slots, range_len,
    coords_hbm, counts, tiles_hbm, rhs_hbm,
    out_ref, phi_ref,
    coords_v, rhs_v, ub, tiles_v, tt, row_ids, col_ids, picks_out, picks_in, c0, c1, d0, d1,
    stats_col, stats_row, m_col, m_full, sub_full, place, placed0, placed1,
    load_sem, send_col, recv_col, send_row, recv_row,
):
    me_p = lax.axis_index("row")
    me_q = lax.axis_index("col")
    per = LANES // slots

    load_rhs = pltpu.make_async_copy(rhs_hbm, rhs_v, load_sem.at[0])
    half = slots // 2
    load_tiles = [
        pltpu.make_async_copy(
            tiles_hbm.at[i * half : (i + 1) * half],
            tiles_v.at[:, :, i * LANES : (i + 1) * LANES],
            load_sem.at[1 + i],
        )
        for i in range(2)
    ]
    load_coords = pltpu.make_async_copy(coords_hbm, coords_v, load_sem.at[3])
    load_coords.start()
    load_rhs.start()
    for load in load_tiles:
        load.start()

    def row_peer(o):
        return (lax.rem(me_p + o, nr), me_q)

    def col_peer(o):
        return (me_p, lax.rem(me_q + o, nc))

    barrier = pltpu.get_barrier_semaphore()
    for o in range(1, nr):
        pl.semaphore_signal(
            barrier, inc=1, device_id=row_peer(o), device_id_type=pl.DeviceIdType.MESH
        )
    for o in range(1, nc):
        pl.semaphore_signal(
            barrier, inc=1, device_id=col_peer(o), device_id_type=pl.DeviceIdType.MESH
        )

    lane = iota((1, LANES), 1)
    load_coords.wait()
    numbers = jnp.concatenate([coords_v[...]] * per, axis=1)
    numbers = jnp.where(iota((2, LANES), 1) % slots < counts[0, 0], numbers, -1).astype(F32)
    row_ids[me_q] = numbers[0:1]
    col_ids[me_p] = numbers[1:2]

    pl.semaphore_wait(barrier, nr + nc - 2)

    sent = []

    def send_over_col(phase, source, mine):
        copies = []
        for o in range(1, nc):
            copy = pltpu.make_async_remote_copy(
                src_ref=source(lax.rem(me_q + o, nc)),
                dst_ref=mine,
                send_sem=send_col.at[phase, o - 1],
                recv_sem=recv_col.at[phase, o - 1],
                device_id=col_peer(o),
                device_id_type=pl.DeviceIdType.MESH,
            )
            copy.start()
            copies.append(copy)
        sent.extend(copies)
        return copies

    def send_over_row(phase, mine):
        copies = []
        for o in range(1, nr):
            copy = pltpu.make_async_remote_copy(
                src_ref=mine,
                dst_ref=mine,
                send_sem=send_row.at[phase, o - 1],
                recv_sem=recv_row.at[phase, o - 1],
                device_id=row_peer(o),
                device_id_type=pl.DeviceIdType.MESH,
            )
            copy.start()
            copies.append(copy)
        sent.extend(copies)
        return copies

    def arrived(copies):
        for copy in copies:
            copy.wait_recv()

    row_ids_copies = send_over_col(0, lambda peer: row_ids.at[me_q], row_ids.at[me_q])
    col_ids_copies = send_over_row(0, col_ids.at[me_p])

    load_rhs.wait()
    squares = []
    for r in range(2):
        part = rhs_v[pl.ds(r, range_len, stride=2), :].astype(BF)
        ub[:, r * LANES : (r + 1) * LANES] = part
        values = part.astype(F32)
        squares.append(total_of(values * values))

    arrived(row_ids_copies)

    def joined(ids_ref, g):
        ids = ids_ref[g * per]
        for j in range(1, per):
            ids = jnp.where(lane // slots == j, ids_ref[g * per + j], ids)
        return ids

    def upright(ids):
        return jnp.broadcast_to(ids, (LANES, LANES)).T

    row_lines = [joined(row_ids, g) for g in range(nc // per)]
    width = min(LANES, range_len)
    base = (me_q * range_len).astype(F32)
    for g in range(nc // per):
        local = upright(row_lines[g] - base)[:, :width]
        column = iota((LANES, width), 1).astype(F32)
        onehot = jnp.concatenate(
            [
                jnp.where(local == column + float(c * width), 1.0, 0.0).astype(BF)
                for c in range(range_len // width)
            ],
            axis=1,
        )
        taken = jnp.dot(onehot, ub[...], preferred_element_type=F32).astype(BF)
        for j in range(per):
            for r in range(2):
                picks_out[g * per + j, r * slots : (r + 1) * slots, :] = taken[
                    j * slots : (j + 1) * slots, r * LANES : (r + 1) * LANES
                ]
    picks_copies = send_over_col(1, lambda peer: picks_out.at[peer], picks_in.at[me_q])
    picks_in[me_q] = picks_out[me_q]

    for s in range(nc // per):
        sub = upright(row_lines[s])
        sub_full[s * LANES : (s + 1) * LANES, :] = sub
        for t in range(nc // per):
            line = row_lines[t]
            m_full[s * LANES : (s + 1) * LANES, t * LANES : (t + 1) * LANES] = jnp.where(
                (sub == line) & (line >= 0.0), 1.0, 0.0
            ).astype(BF)
    own_rows = pl.ds(pl.multiple_of(me_q * slots, slots), slots)
    m_row = m_full[own_rows, :]
    row_live = sub_full[own_rows, :] >= 0.0

    for load in load_tiles:
        load.wait()

    def turn(first, last):
        for k in range(first, last):
            for i in range(2):
                lanes = slice(i * LANES, (i + 1) * LANES)
                tt[k * LANES : (k + 1) * LANES, lanes] = (
                    tiles_v[k, :, lanes].astype(F32).T.astype(BF)
                )

    turn(0, half // 2)
    stacked = tiles_v[...].reshape(half * LANES, 2 * LANES)

    def over_row(phase, buffer, r, values, blocks):
        own = diagonal_dot(values, blocks, slots).astype(BF)
        buffer[r, me_p] = own
        return own, send_over_row(phase + r, buffer.at[r, me_p])

    def over_col(phase, buffer, r, values, blocks):
        own = diagonal_dot(values, blocks, slots).astype(BF)
        buffer[r, me_q] = own
        return own, send_over_col(
            phase + r, lambda peer: buffer.at[r, me_q], buffer.at[r, me_q]
        )

    def total(matches, buffer, r):
        return jnp.dot(
            matches, buffer[r].reshape(-1, LANES), preferred_element_type=F32
        )

    def inner(own, summed, live):
        return total_of(jnp.where(live, own.astype(F32) * summed, 0.0))

    arrived(picks_copies)
    c0_sent = []
    for r in range(2):
        u0 = picks_in[0, r * slots : (r + 1) * slots, :].astype(F32)
        for j in range(1, nc):
            u0 = u0 + picks_in[j, r * slots : (r + 1) * slots, :].astype(F32)
        c0_sent.append(over_row(1, c0, r, u0, stacked))

    turn(half // 2, half)
    arrived(col_ids_copies)
    sub_col = upright(col_ids[me_p])[:slots]
    col_live = sub_col >= 0.0
    col_lines = [joined(col_ids, g) for g in range(nr // per)]
    for s in range(nr // per):
        line = col_lines[s]
        m_col[:, s * LANES : (s + 1) * LANES] = jnp.where(
            (sub_col == line) & (line >= 0.0), 1.0, 0.0
        ).astype(BF)
    col_base = (me_p * range_len).astype(F32)
    chunk = min(256, range_len)
    for start in range(0, range_len, chunk):
        number = (iota((chunk, LANES), 0) + start).astype(F32)
        for s in range(nr // per):
            place[start : start + chunk, s * LANES : (s + 1) * LANES] = jnp.where(
                number == col_lines[s] - col_base, 1.0, 0.0
            ).astype(BF)

    def put(buffer, target):
        both = jnp.concatenate([buffer[r].reshape(nr * slots, LANES) for r in range(2)], axis=1)
        for start in range(0, range_len, chunk):
            target[start : start + chunk, :] = jnp.dot(
                place[start : start + chunk, :], both, preferred_element_type=F32
            )

    g0, d0_sent = [], []
    for r in range(2):
        arrived(c0_sent[r][1])
        g0.append(total(m_col[...], c0, r))
        d0_sent.append(over_col(2, d0, r, g0[r], tt[...]))
    gg = [inner(c0_sent[r][0], g0[r], col_live) for r in range(2)]

    f0, c1_sent = [], []
    for r in range(2):
        arrived(d0_sent[r][1])
        f0.append(total(m_row, d0, r))
        c1_sent.append(over_row(3, c1, r, f0[r], stacked))
    ff = [inner(d0_sent[r][0], f0[r], row_live) for r in range(2)]
    put(c0, placed0)

    g1, d1_sent = [], []
    for r in range(2):
        arrived(c1_sent[r][1])
        g1.append(total(m_col[...], c1, r))
        d1_sent.append(over_col(4, d1, r, g1[r], tt[...]))
    hh = [inner(c1_sent[r][0], g1[r], col_live) for r in range(2)]

    stats = jnp.zeros((1, LANES), F32)
    for s, pair in enumerate((squares, gg, ff, hh)):
        for r in range(2):
            stats = jnp.where(lane == 2 * s + r, pair[r], stats)
    stats_col[me_q] = stats
    stats_col_copies = send_over_col(6, lambda peer: stats_col.at[me_q], stats_col.at[me_q])

    full_live = sub_full[...] >= 0.0
    ee = []
    for r in range(2):
        arrived(d1_sent[r][1])
        f1 = total(m_full[...], d1, r)
        ee.append(inner(d1[r].reshape(nc * slots, LANES), f1, full_live))
    arrived(stats_col_copies)
    group = jnp.sum(stats_col[...], axis=0)
    for r in range(2):
        group = jnp.where(lane == 8 + r, ee[r], group)
    stats_row[me_p] = group
    earlier = list(sent)
    stats_row_copies = send_over_row(5, stats_row.at[me_p])
    put(c1, placed1)
    for copy in earlier:
        copy.wait_send()
    arrived(stats_row_copies)
    whole = jnp.sum(stats_row[...], axis=0)

    uu, gg, ff, hh, ee = [whole] + [pltpu.roll(whole, LANES - 2 * s, 1) for s in range(1, 5)]

    def norm(square):
        return jnp.sqrt(jnp.maximum(square, 0.0) + EPS)

    beta0 = norm(uu)
    alpha0 = norm(gg / (beta0 * beta0))
    a = 1.0 / (beta0 * alpha0)
    b = alpha0 / beta0
    beta1 = norm(a * a * ff - 2.0 * (a * b) * gg + b * b * uu)
    rho0 = jnp.sqrt(alpha0 * alpha0 + beta1 * beta1)
    cosine = alpha0 / rho0
    sine = beta1 / rho0
    phi0 = cosine * beta0
    phi_bar = sine * beta0
    x = a / beta1
    y = -(b / beta1 + beta1 * a)
    alpha1 = norm(x * x * hh + 2.0 * (x * y) * ff + y * y * gg)
    theta = sine * alpha1
    rho_bar = -cosine * alpha1
    e = x / alpha1
    h = y / alpha1 - (alpha1 / beta1) * a
    w = (alpha1 / beta1) * b
    beta2 = norm(
        e * e * ee + h * h * ff + w * w * uu
        + 2.0 * (e * h) * hh + 2.0 * (e * w) * ff + 2.0 * (h * w) * gg
    )
    rho1 = jnp.sqrt(rho_bar * rho_bar + beta2 * beta2)
    phi1 = (rho_bar / rho1) * phi_bar
    phi_ref[...] = ((beta2 / rho1) * phi_bar)[:, 0:2]
    on_g1 = (phi1 / rho1) * e
    on_g0 = (phi0 / rho0) * a + (phi1 / rho1) * (y / alpha1 - (theta / rho0) * a)

    for start in range(0, range_len, chunk):
        here = slice(start, start + chunk)
        for r in range(2):
            lanes = slice(r * LANES, (r + 1) * LANES)
            out_ref[pl.ds(2 * start + r, chunk, stride=2), :] = (
                placed0[here, lanes] * on_g0[:, r : r + 1]
                + placed1[here, lanes] * on_g1[:, r : r + 1]
            )

    for copy in stats_row_copies:
        copy.wait_send()


def on_device(nr, nc, tiles, coords, counts, rhs):
    slots, block = tiles.shape[2], tiles.shape[3]
    range_len = rhs.shape[1] // block
    piece = rhs.reshape(2, range_len, block).transpose(1, 0, 2).reshape(2 * range_len, block)
    dma = pltpu.SemaphoreType.DMA
    placed, phi = pl.pallas_call(
        functools.partial(solver, nr, nc, slots, range_len),
        out_shape=(
            jax.ShapeDtypeStruct((2 * range_len, block), F32),
            jax.ShapeDtypeStruct((1, 2), F32),
        ),
        in_specs=[
            pl.BlockSpec(memory_space=pltpu.HBM),
            pl.BlockSpec(memory_space=pltpu.SMEM),
            pl.BlockSpec(memory_space=pltpu.HBM),
            pl.BlockSpec(memory_space=pltpu.HBM),
        ],
        out_specs=(
            pl.BlockSpec(memory_space=pltpu.VMEM),
            pl.BlockSpec(memory_space=pltpu.VMEM),
        ),
        scratch_shapes=[
            pltpu.VMEM((2, slots), jnp.int32),
            pltpu.VMEM((2 * range_len, block), F32),
            pltpu.VMEM((range_len, 2 * block), BF),
            pltpu.VMEM((slots // 2, block, 2 * block), BF),
            pltpu.VMEM((slots // 2 * block, 2 * block), BF),
            pltpu.VMEM((nc, 1, LANES), F32),
            pltpu.VMEM((nr, 1, LANES), F32),
            pltpu.VMEM((nc, 2 * slots, block), BF),
            pltpu.VMEM((nc, 2 * slots, block), BF),
            pltpu.VMEM((2, nr, slots, block), BF),
            pltpu.VMEM((2, nr, slots, block), BF),
            pltpu.VMEM((2, nc, slots, block), BF),
            pltpu.VMEM((2, nc, slots, block), BF),
            pltpu.VMEM((nc, 1, LANES), F32),
            pltpu.VMEM((nr, 1, LANES), F32),
            pltpu.VMEM((slots, nr * slots), BF),
            pltpu.VMEM((nc * slots, nc * slots), BF),
            pltpu.VMEM((nc * slots, LANES), F32),
            pltpu.VMEM((range_len, nr * slots), BF),
            pltpu.VMEM((range_len, 2 * block), F32),
            pltpu.VMEM((range_len, 2 * block), F32),
            dma((4,)),
            dma((7, nc - 1)),
            dma((7, nc - 1)),
            dma((6, nr - 1)),
            dma((6, nr - 1)),
        ],
        compiler_params=pltpu.CompilerParams(
            collective_id=0, has_side_effects=True, vmem_limit_bytes=48 * 1024 * 1024
        ),
    )(
        pltpu.with_memory_space_constraint(coords[0, 0].T, pltpu.HBM),
        counts,
        pltpu.with_memory_space_constraint(tiles[0, 0], pltpu.HBM),
        pltpu.with_memory_space_constraint(piece, pltpu.HBM),
    )
    answer = placed.reshape(range_len, 2, block).transpose(1, 0, 2).reshape(2, range_len * block)
    return answer, phi[0]


def solution(mesh):
    nr, nc = mesh.shape["row"], mesh.shape["col"]
    return jax.shard_map(
        functools.partial(on_device, nr, nc),
        mesh=mesh,
        in_specs=(
            P("row", "col", None, None, None),
            P("row", "col", None, None),
            P("row", "col"),
            P(None, ("row", "col")),
        ),
        out_specs=(P(None, ("col", "row")), P()),
        check_vma=False,
    )
```
